32 devices in a mesh: req: 16 (over z, x, core), head: 2 (over y).
Axes of the slice: x: 2, y: 2, z: 4, core: 2. Of those that a mesh axis runs over, the one named last changes fastest.
Arguments:
- tokens: bfloat16 [16, 512, 1024], P('req', 'head'), may hold values from -6 to 6
- gain: bfloat16 [1024], replicated, may hold values from 0.099609375 to 1.8984375
- projection_weight: bfloat16 [1024, 4, 1024], P(None, None, 'head'), may hold values from -0.1875 to 0.1875
- output_weight: bfloat16 [1024, 1024], P('head'), may hold values from -0.1875 to 0.1875
- persist: bfloat16 [2, 16, 1024], P(None, None, 'head'), may hold values from -6 to 6
- cache_page_slots: bfloat16 [16, 16, 256, 2, 1024], P('req', None, None, None, 'head'), may hold values from -250 to 250
- cached_length: int32 [16], P('req'), may hold values from 225 to 4096, as said below
- page_keeper: int32 [16, 128], P('req'), may hold values from -1 to 15, as said below
- page_slot_index: int32 [16, 128], P('req'), may hold values from -1 to 7, as said below
- memory_state: float32 [2, 16, 8, 128, 128], P(None, 'req', 'head'), may hold values from -3 to 3
- retention: float32 [16, 8], P('req', 'head'), may hold values from 0.2 to 1
- momentum: float32 [16, 8], P('req', 'head'), may hold values from 0.2 to 0.9
- memory_step_scale: float32 [16, 8], P('req', 'head'), may hold values from 0.02 to 0.3
- halving_updates: int32 [16, 8], P('req'), may hold values 0 or 1
Outputs:
- layer_out: bfloat16 [16, 512, 1024], P('req', 'head')
- new_state: float32 [2, 16, 8, 128, 128], P(None, 'req', 'head')
The draws below stay inside these ranges and needn't reach their ends.
Inputs may be any that keep to these rules, and one draw needn't show every extreme that they name: `cached_length`: the requests of one device hold together at most 128 pages. `page_keeper`: pages j below cached_length[r] / 32 (rounded up) have a keeper; later entries are -1. No keeper and slot serve two pages of the requests of one device. `page_slot_index`: -1 exactly where page_keeper is -1.
All inputs are finite; a program needn't handle non-finite values. No bound on the sum of `halving_updates` on one device may be relied on, other than what follows from the above.
Results may differ from the reference program's by a relative error of at most 0.012.
The reference program's roundings to bfloat16 on the way count: a program that leaves them out, or rounds other values in their place, can miss the bound.
Values may be sent and summed in bfloat16 or wider, within the bound.
No kernel may reach another device: no remote copies, remote signals or barrier semaphores. Data moves between devices by JAX's collectives and lax.ppermute only.
A program may use at most 128 MiB of HBM per device.

```python
import math
import jax
import jax.numpy as jnp
from jax import lax

D = 1024
H = 8
HD = 128
PERSIST = 16
BLK = 64
PREFILL = 512
PAGE = 32
REQ_DEV = 1
REQUEST_TOTAL = 16
MAXPAGES = 128
CAP = 8
UPDATE_BLOCKS = 8
N_HEAD = 2


def layout_tables(key):
    base = jax.random.fold_in(key, 7)
    first, second, third, fourth = jax.random.split(base, 4)
    homes = REQUEST_TOTAL // REQ_DEV
    bound = MAXPAGES + (REQ_DEV - 1) * (MAXPAGES // 2)
    raw_pages = jax.random.randint(first, (homes, REQ_DEV), CAP, MAXPAGES + 1)
    columns_list = []
    running = jnp.zeros((homes,), jnp.int32)
    for which in range(REQ_DEV):
        room = bound - running - (REQ_DEV - 1 - which) * CAP
        taken = jnp.minimum(raw_pages[:, which], room).astype(jnp.int32)
        columns_list.append(taken)
        running = running + taken
    pages = jnp.stack(columns_list, axis=1)
    chosen = jax.random.randint(second, (), 0, homes)
    forced = jnp.where(jnp.arange(REQ_DEV) == 0, MAXPAGES, MAXPAGES // 2).astype(jnp.int32)
    is_chosen = jnp.arange(homes)[:, None] == chosen
    pages = jnp.where(is_chosen, forced[None, :], pages)
    trims = jax.random.randint(third, (homes, REQ_DEV), 0, PAGE)
    trims = jnp.where(is_chosen & (jnp.arange(REQ_DEV)[None, :] == 0), 0, trims)
    lengths = (pages * PAGE - trims).reshape(REQUEST_TOTAL).astype(jnp.int32)
    before = jnp.cumsum(pages, axis=1) - pages
    keepers = jax.vmap(lambda single: jax.random.permutation(single, homes))(jax.random.split(fourth, homes))
    page_ids = jnp.arange(MAXPAGES)
    slot = before[:, :, None] + page_ids[None, None, :]
    used = page_ids[None, None, :] < pages[:, :, None]
    owners = jnp.take_along_axis(keepers, (slot % homes).reshape(homes, REQ_DEV * MAXPAGES), axis=1).reshape(homes, REQ_DEV, MAXPAGES)
    owners = jnp.where(used, owners, -1).reshape(REQUEST_TOTAL, MAXPAGES).astype(jnp.int32)
    lanes = jnp.where(used, slot // homes, -1).reshape(REQUEST_TOTAL, MAXPAGES).astype(jnp.int32)
    return (lengths, owners, lanes)


def draw_cached_length(key, part):
    return layout_tables(key)[0]


def draw_page_keeper(key, part):
    return layout_tables(key)[1]


def draw_page_slot_index(key, part):
    return layout_tables(key)[2]


def draw_cache_page_slots(key, part):
    homes = REQUEST_TOTAL // REQ_DEV
    span = CAP * PAGE
    shape = (homes, homes, span // 2, 2, 2, H * HD)
    first, second = jax.random.split(key, 2)
    base = jnp.clip(1.5 * jax.random.normal(first, shape, jnp.float32), -6.0, 6.0)
    chosen = jax.random.randint(second, (homes, homes, span // 2), 0, 1024) == 0
    lead_key = base[:, :, :, 0, 0, :]
    boosted = jnp.stack([40.0 * lead_key, 40.4 * lead_key], axis=3)
    keys_new = jnp.where(chosen[:, :, :, None, None], boosted, base[:, :, :, :, 0, :])
    result = jnp.stack([keys_new, base[:, :, :, :, 1, :]], axis=4).reshape(homes, homes, span, 2, H * HD)
    return result.astype(jnp.bfloat16)


def set_ends(array, own_key, low, top_value):
    longest = array.shape.index(max(array.shape))
    spots = []
    for shift in (0, 1):
        where = [jax.random.randint(jax.random.fold_in(own_key, axis), (), 0, length) for axis, length in enumerate(array.shape)]
        where[longest] = (where[longest] + shift) % array.shape[longest]
        spots.append(tuple(where))
    return array.at[spots[0]].set(low).at[spots[1]].set(top_value)


def steps_of(rng, dims, pieces, smallest, largest):
    level = 1.0
    for dim, parts in pieces:
        draws = jax.random.uniform(jax.random.fold_in(jax.random.fold_in(rng, 6), dim), (parts,), jnp.float32, smallest / len(pieces), largest / len(pieces))
        level = level * jnp.repeat(jnp.exp(draws), dims[dim] // parts).reshape((-1,) + (1,) * (len(dims) - 1 - dim))
    return level


def scatter_about(own_key, dims, deviation, most, pieces=(), kind=jnp.bfloat16):
    array = jax.random.normal(own_key, dims, jnp.float32) * deviation
    if len(pieces) > 0:
        array = steps_of(own_key, dims, pieces, -0.22, 0.18) * array
    return jnp.clip(array, min=-most, max=most).astype(kind)


def setup_inputs(seed: int = 0) -> dict:
    splits = jax.random.split(jax.random.key(seed), 15)
    tokens = scatter_about(splits[0], (REQUEST_TOTAL, PREFILL, D), 1.0, 6.0, ((0, 16), (1, 2)))
    gain = jnp.clip(1.0 + 0.18 * jax.random.normal(splits[1], (D,), jnp.float32), 0.099609375, 1.8984375).astype(jnp.bfloat16)
    projection_weight = scatter_about(splits[2], (D, 4, H * HD), D ** -0.5, 0.1875, ((2, 2),))
    output_weight = scatter_about(splits[3], (H * HD, D), (H * HD) ** -0.5, 0.1875, ((0, 2),))
    persist = scatter_about(splits[4], (2, PERSIST, H * HD), 1.0, 6.0, ((2, 2),))
    cache_page_slots = draw_cache_page_slots(jax.random.fold_in(splits[14], 71), 0)
    cached_length = draw_cached_length(jax.random.fold_in(splits[14], 71), 0)
    page_keeper = draw_page_keeper(jax.random.fold_in(splits[14], 71), 0)
    page_slot_index = draw_page_slot_index(jax.random.fold_in(splits[14], 71), 0)
    memory_state = scatter_about(splits[9], (2, REQUEST_TOTAL, H, HD, HD), 0.5, 3.0, ((1, 16), (2, 2)), jnp.float32)
    retention = jnp.clip(jnp.exp(math.log(1.0) - 1.609438 * jax.random.uniform(splits[10], (REQUEST_TOTAL, H), jnp.float32) ** steps_of(splits[10], (REQUEST_TOTAL, H), ((0, 16), (1, 2)), -0.2, 0.2)), 0.2, 1.0)
    momentum = jnp.clip(0.2 + 0.7 * jax.random.uniform(splits[11], (REQUEST_TOTAL, H), jnp.float32) ** steps_of(splits[11], (REQUEST_TOTAL, H), ((0, 16), (1, 2)), -0.2, 0.2), 0.2, 0.9)
    memory_step_scale = jnp.clip(jnp.exp(math.log(0.3) - 2.7080503 * jax.random.uniform(splits[12], (REQUEST_TOTAL, H), jnp.float32) ** steps_of(splits[12], (REQUEST_TOTAL, H), ((0, 16), (1, 2)), -0.2, 0.2)), 0.02, 0.3)
    halving_updates = set_ends((jax.random.randint(splits[13], (REQUEST_TOTAL, UPDATE_BLOCKS), 0, 4) < 1).astype(jnp.int32), jax.random.fold_in(splits[13], 1), 0, 1)
    return dict(tokens=tokens, gain=gain, projection_weight=projection_weight, output_weight=output_weight, persist=persist, cache_page_slots=cache_page_slots, cached_length=cached_length, page_keeper=page_keeper, page_slot_index=page_slot_index, memory_state=memory_state, retention=retention, momentum=momentum, memory_step_scale=memory_step_scale, halving_updates=halving_updates)


norm_eps = 1e-05
unit_eps = 1e-06

def unit_rows(values_f):
    return values_f * lax.rsqrt(lax.optimization_barrier(jnp.sum(values_f * values_f, axis=-1, keepdims=True)) + unit_eps)

def reference(tokens, gain, projection_weight, output_weight, persist, cache_page_slots, cached_length, page_keeper, page_slot_index, memory_state, retention, momentum, memory_step_scale, halving_updates):
    columns = H * HD
    homes = REQUEST_TOTAL // REQ_DEV
    scale = 1.0 / math.sqrt(HD)
    highest = lax.Precision.HIGHEST
    flat_w = projection_weight.reshape(D, 4 * columns)
    gain_f = gain.astype(jnp.float32)
    causal = jnp.arange(PREFILL)[:, None] >= jnp.arange(PREFILL)[None, :]
    slot_ids = jnp.arange(homes * CAP, dtype=jnp.int32)
    page_ids = jnp.arange(MAXPAGES, dtype=jnp.int32)
    position = jnp.arange(PAGE, dtype=jnp.int32)
    group_w = output_weight.reshape(N_HEAD, columns // N_HEAD, D).astype(jnp.float32)
    persist_keys = persist[0].reshape(PERSIST, H, HD).astype(jnp.float32)
    persist_values = persist[1].reshape(PERSIST, H, HD).astype(jnp.float32)

    def one_request(index_value):
        inputs = tokens[index_value].astype(jnp.float32)
        normed = (inputs * lax.rsqrt(lax.optimization_barrier(jnp.mean(inputs * inputs, axis=-1, keepdims=True)) + norm_eps) * gain_f).astype(jnp.bfloat16)
        projected = jnp.dot(normed, flat_w, preferred_element_type=jnp.float32).reshape(PREFILL, 4, H, HD)
        rounded = (projected[:, 0].astype(jnp.bfloat16), projected[:, 1].astype(jnp.bfloat16), projected[:, 2].astype(jnp.bfloat16))
        rounded = lax.optimization_barrier(rounded)
        queries = rounded[0].astype(jnp.float32)
        own_keys = rounded[1].astype(jnp.float32)
        own_values = rounded[2].astype(jnp.float32)
        gate = projected[:, 3]
        pool = lax.dynamic_index_in_dim(cache_page_slots, index_value // REQ_DEV, axis=1, keepdims=False)
        cache_keys = pool[:, :, 0].reshape(homes * CAP * PAGE, H, HD).astype(jnp.float32)
        cache_values = pool[:, :, 1].reshape(homes * CAP * PAGE, H, HD).astype(jnp.float32)
        filled = jnp.clip(cached_length[index_value] - page_ids * PAGE, 0, PAGE)
        slot_of = page_keeper[index_value] * CAP + page_slot_index[index_value]
        slot_fill = lax.optimization_barrier(jnp.sum(jnp.where(slot_of[:, None] == slot_ids[None, :], filled[:, None], 0), axis=0))
        valid = (position[None, :] < slot_fill[:, None]).reshape(homes * CAP * PAGE)
        score_p = jnp.einsum('thc,khc->thk', queries, persist_keys) * scale
        score_c = jnp.where(valid[None, None, :], jnp.einsum('thc,khc->thk', queries, cache_keys) * scale, -jnp.inf)
        score_t = jnp.where(causal[:, None, :], jnp.einsum('thc,khc->thk', queries, own_keys) * scale, -jnp.inf)
        row_max = jnp.maximum(jnp.maximum(lax.optimization_barrier(jnp.max(score_p, axis=-1, keepdims=True)), lax.optimization_barrier(jnp.max(score_c, axis=-1, keepdims=True))), lax.optimization_barrier(jnp.max(score_t, axis=-1, keepdims=True)))
        exp_p = jnp.exp(score_p - row_max)
        exp_c = jnp.exp(score_c - row_max)
        exp_t = jnp.exp(score_t - row_max)
        total = lax.optimization_barrier(jnp.sum(exp_p, axis=-1, keepdims=True)) + lax.optimization_barrier(jnp.sum(exp_c, axis=-1, keepdims=True)) + lax.optimization_barrier(jnp.sum(exp_t, axis=-1, keepdims=True))
        weight_set = lax.optimization_barrier((exp_p.astype(jnp.bfloat16), exp_c.astype(jnp.bfloat16), exp_t.astype(jnp.bfloat16)))
        mixed = jnp.einsum('thk,khc->thc', weight_set[0].astype(jnp.float32), persist_values)
        mixed = mixed + jnp.einsum('thk,khc->thc', weight_set[1].astype(jnp.float32), cache_values)
        mixed = mixed + jnp.einsum('thk,khc->thc', weight_set[2].astype(jnp.float32), own_values)
        attended = mixed / total
        unit_attn = attended * lax.rsqrt(lax.optimization_barrier(jnp.mean(attended * attended, axis=-1, keepdims=True)) + unit_eps)
        query_unit = unit_rows(queries)
        key_unit = unit_rows(own_keys)
        state_m = memory_state[0, index_value]
        state_s = memory_state[1, index_value]
        rate_values = retention[index_value]
        pushes = momentum[index_value]
        strides = memory_step_scale[index_value]
        reads = []
        for block_span in range(UPDATE_BLOCKS):
            lower = block_span * BLK
            q_block = query_unit[lower:lower + BLK]
            k_block = key_unit[lower:lower + BLK]
            v_block = own_values[lower:lower + BLK]
            reads.append(jnp.einsum('thc,hdc->thd', q_block, state_m, precision=highest))
            errors = jnp.einsum('thc,hdc->thd', k_block, state_m, precision=highest) - v_block
            grads = jnp.einsum('thd,thc->hdc', errors, k_block, precision=highest)
            state_s = pushes[:, None, None] * state_s - strides[:, None, None] * grads
            keeper_list = rate_values * jnp.where(halving_updates[index_value, block_span] == 1, 0.5, 1.0)
            state_m = keeper_list[:, None, None] * state_m + state_s
        memory_read = jnp.concatenate(reads, axis=0)
        head_out = (unit_attn + jax.nn.sigmoid(gate) * memory_read).astype(jnp.bfloat16)
        head_out = lax.optimization_barrier(head_out)
        grouped = head_out.reshape(PREFILL, N_HEAD, columns // N_HEAD).astype(jnp.float32)
        partials = jnp.einsum('tgc,gcd->tgd', grouped, group_w).astype(jnp.bfloat16)
        partials = lax.optimization_barrier(partials)
        layer_out = lax.optimization_barrier(jnp.sum(partials.astype(jnp.float32), axis=1)).astype(jnp.bfloat16)
        return (layer_out, jnp.stack([state_m, state_s]))
    outputs, states = lax.map(one_request, jnp.arange(REQUEST_TOTAL, dtype=jnp.int32))
    return (outputs, jnp.transpose(states, (1, 0, 2, 3, 4)))
```

```python
import functools
import math

import jax
import jax.numpy as jnp
from jax import lax
from jax.experimental import pallas as pl
from jax.experimental.layout import Layout, with_layout_constraint
from jax.experimental.pallas import tpu as pltpu
from jax.sharding import PartitionSpec as P

HD = 128
BLK = 64
PAGE = 32
GROUP = 4


norm_eps = 1e-05
unit_eps = 1e-06
LOG2E = math.log2(math.e)
MASKED = -1e30
TAIL = 16
f32 = jnp.float32
bf16 = jnp.bfloat16


def dot(left, right, contract=((1,), (0,)), precision=None):
    return lax.dot_general(
        left, right, (contract, ((), ())), precision=precision, preferred_element_type=f32
    )


def as_it_lies(value):
    return with_layout_constraint(value, Layout(major_to_minor=tuple(range(value.ndim))))


def cache_kernel(shape, sent, at_ref, fill_ref, after_ref, *refs):
    del at_ref, after_ref
    span, lanes, count, parts = shape
    q_refs, kv_refs = refs[:parts], refs[parts : parts + count]
    outs = refs[parts + count : -2]
    bias_ref, score_ref = refs[-2:]
    scale = LOG2E / math.sqrt(HD)

    @pl.when(pl.program_id(0) == 0)
    def _():
        row = lax.broadcasted_iota(jnp.int32, (PAGE, HD), 0)
        for g in range(count):
            for l in range(lanes):
                bias_ref[pl.ds(g * span + l * PAGE, PAGE), :] = jnp.where(
                    row < fill_ref[g, l], 0.0, MASKED
                )

    q = jnp.concatenate([ref[...] for ref in q_refs], axis=1)
    tokens = q.shape[1]
    top = jnp.full((1, tokens), MASKED, f32)
    for g in range(count):
        rows = pl.ds(g * span, span)
        score = dot(kv_refs[g][0, 0], q) * scale + jnp.tile(bias_ref[rows, :], (1, tokens // HD))
        score_ref[rows, :] = score
        top = jnp.maximum(top, jnp.max(score, axis=0, keepdims=True))
    total = jnp.zeros((1, tokens), f32)
    mixed = jnp.zeros((HD, tokens), f32)
    for g in range(count):
        rows = pl.ds(g * span, span)
        weight = jnp.exp2(score_ref[rows, :] - top)
        total = total + jnp.sum(weight, axis=0, keepdims=True)
        mixed = mixed + dot(kv_refs[g][0, 1], weight.astype(bf16), ((0,), (0,)))
    attended = mixed / total
    lse = top + jnp.log2(total)
    if sent:
        high = lse.astype(bf16).astype(f32)
        middle = (lse - high).astype(bf16).astype(f32)
        terms = [high, middle, lse - high - middle, jnp.zeros((TAIL - 3, tokens), f32)]
        outs[0][0] = jnp.concatenate([attended] + terms, axis=0).astype(bf16)
    else:
        outs[0][0] = attended
        outs[1][0] = lse


def cache_attention(fill, queries, kvs, at, sent, after):
    count = len(kvs)
    cols = kvs[0].shape[3]
    span = kvs[0].shape[2]
    heads = cols // HD
    tokens = sum(q.shape[1] for q in queries)

    def head_spec(*block):
        return pl.BlockSpec((1,) + block, lambda h, at, fill: (h, 0, 0))

    if sent:
        out_shape = (jax.ShapeDtypeStruct((heads, HD + TAIL, tokens), bf16),)
        out_specs = (head_spec(HD + TAIL, tokens),)
    else:
        out_shape = (
            jax.ShapeDtypeStruct((heads, HD, tokens), f32),
            jax.ShapeDtypeStruct((heads, 1, tokens), f32),
        )
        out_specs = (head_spec(HD, tokens), head_spec(1, tokens))
    return pl.pallas_call(
        functools.partial(cache_kernel, (span, span // PAGE, count, len(queries)), sent),
        out_shape=out_shape,
        grid_spec=pltpu.PrefetchScalarGridSpec(
            num_scalar_prefetch=2,
            grid=(heads,),
            in_specs=[pl.BlockSpec(memory_space=pl.ANY)]
            + [pl.BlockSpec((HD, q.shape[1]), lambda h, at, fill: (h, 0)) for q in queries]
            + [
                pl.BlockSpec((1, 2, span, HD), lambda h, at, fill, g=g: (at[g], 0, 0, h))
                for g in range(count)
            ],
            out_specs=out_specs,
            scratch_shapes=[
                pltpu.VMEM((count * span, HD), f32),
                pltpu.VMEM((count * span, tokens), f32),
            ],
        ),
        compiler_params=pltpu.CompilerParams(vmem_limit_bytes=32 * 2**20),
        cost_estimate=pl.CostEstimate(
            flops=4 * cols * tokens * count * span,
            bytes_accessed=4 * count * span * cols + 4 * cols * tokens,
            transcendentals=heads * tokens * count * span,
        ),
    )(jnp.stack(at), fill, after, *queries, *kvs)


def own_kernel(shard, shards_in_all, side_ref, q_ref, k_ref, v_ref, persist_ref, att_ref, lse_ref):
    def place(axis):
        at = lax.broadcasted_iota(jnp.int32, (tokens, tokens), axis)
        return lax.rem(side_ref[0] + at // shard, shards_in_all) * shard + lax.rem(at, shard)

    scale = LOG2E / math.sqrt(HD)
    q = q_ref[...]
    tokens = q.shape[1]
    score_p = dot(persist_ref[0], q) * scale
    score_t = dot(k_ref[...].T, q) * scale
    score_t = jnp.where(place(0) <= place(1), score_t, MASKED)
    top = jnp.maximum(
        jnp.max(score_p, axis=0, keepdims=True), jnp.max(score_t, axis=0, keepdims=True)
    )
    weight_p = jnp.exp2(score_p - top)
    weight_t = jnp.exp2(score_t - top)
    total = jnp.sum(weight_p, axis=0, keepdims=True) + jnp.sum(weight_t, axis=0, keepdims=True)
    mixed = dot(v_ref[...], weight_t.astype(bf16)) + dot(
        persist_ref[1], weight_p.astype(bf16), ((0,), (0,))
    )
    att_ref[0] = mixed / total
    lse_ref[0] = top + jnp.log2(total)


def own_attention(side, shard, q, k, v, persist):
    cols, tokens = q.shape
    heads = cols // HD
    head_spec = pl.BlockSpec((HD, tokens), lambda h: (h, 0))
    return pl.pallas_call(
        functools.partial(own_kernel, shard, tokens // shard),
        out_shape=(
            jax.ShapeDtypeStruct((heads, HD, tokens), f32),
            jax.ShapeDtypeStruct((heads, 1, tokens), f32),
        ),
        grid=(heads,),
        in_specs=[pl.BlockSpec(memory_space=pltpu.SMEM)]
        + [head_spec] * 3
        + [pl.BlockSpec((2, persist.shape[1], HD), lambda h: (0, 0, h))],
        out_specs=(
            pl.BlockSpec((1, HD, tokens), lambda h: (h, 0, 0)),
            pl.BlockSpec((1, 1, tokens), lambda h: (h, 0, 0)),
        ),
        compiler_params=pltpu.CompilerParams(vmem_limit_bytes=32 * 2**20),
        cost_estimate=pl.CostEstimate(
            flops=4 * cols * tokens * tokens,
            bytes_accessed=10 * cols * tokens,
            transcendentals=heads * tokens * tokens,
        ),
    )(side[None], q, k, v, persist)


def memory_kernel(
    retention_ref, momentum_ref, step_ref, halving_ref, q_ref, k_ref, v_ref, state_ref,
    read_ref, new_ref, kn_ref,
):
    heads = state_ref.shape[1]
    tokens = q_ref.shape[1]
    exact = lax.Precision.HIGHEST
    units = []
    for h in range(heads):
        rows = pl.ds(h * HD, HD)
        q = q_ref[rows, :].astype(f32)
        k = k_ref[rows, :].astype(f32)
        qn = q * lax.rsqrt(jnp.sum(q * q, axis=0, keepdims=True) + unit_eps)
        kn = k * lax.rsqrt(jnp.sum(k * k, axis=0, keepdims=True) + unit_eps)
        kn_ref[h] = kn.T
        units.append((qn, kn))
    ms = [state_ref[0, h] for h in range(heads)]
    ss = [state_ref[1, h] for h in range(heads)]
    for b in range(tokens // BLK):
        lower, upper = b * BLK, (b + 1) * BLK
        for h in range(heads):
            rows = pl.ds(h * HD, HD)
            qn, kn = units[h]
            both = jnp.concatenate([kn[:, lower:upper], qn[:, lower:upper]], axis=1)
            product = dot(ms[h], both, precision=exact)
            error = product[:, :BLK] - v_ref[rows, lower:upper].astype(f32)
            read_ref[rows, lower:upper] = product[:, BLK:]
            grad = dot(error, kn_ref[h, lower:upper, :], precision=exact)
            ss[h] = momentum_ref[0, h] * ss[h] - step_ref[0, h] * grad
            keep = retention_ref[0, h] * jnp.where(halving_ref[0, b] == 1, 0.5, 1.0)
            ms[h] = keep * ms[h] + ss[h]
    for h in range(heads):
        new_ref[0, h] = ms[h]
        new_ref[1, h] = ss[h]


def memory_pass(retention, momentum, step, halving, q, k, v, state):
    cols, tokens = q.shape
    heads = cols // HD
    smem = pl.BlockSpec(memory_space=pltpu.SMEM)
    vmem = pl.BlockSpec(memory_space=pltpu.VMEM)
    return pl.pallas_call(
        memory_kernel,
        out_shape=(
            jax.ShapeDtypeStruct((cols, tokens), f32),
            jax.ShapeDtypeStruct(state.shape, f32),
        ),
        in_specs=[smem] * 4 + [vmem] * 4,
        out_specs=(vmem, vmem),
        scratch_shapes=[pltpu.VMEM((heads, tokens, HD), f32)],
        compiler_params=pltpu.CompilerParams(vmem_limit_bytes=32 * 2**20),
        cost_estimate=pl.CostEstimate(
            flops=60 * cols * tokens * HD, bytes_accessed=10 * cols * tokens, transcendentals=0
        ),
    )(retention, momentum, step, halving, q, k, v, state)


def merge_kernel(near, far, *refs):
    pairs = [(refs[2 * i][0], refs[2 * i + 1][0]) for i in range(near)]
    for ref in refs[2 * near : 2 * near + far]:
        lse = jnp.sum(ref[0, HD:, :].astype(f32), axis=0, keepdims=True)
        pairs.append((ref[0, :HD, :].astype(f32), lse))
    gate_ref, read_ref, out_ref = refs[2 * near + far :]
    top = functools.reduce(jnp.maximum, [lse for _, lse in pairs])
    total = jnp.zeros_like(top)
    mixed = jnp.zeros(out_ref.shape, f32)
    for att, lse in pairs:
        share = jnp.exp2(lse - top)
        total = total + share
        mixed = mixed + att * share
    attended = mixed / total
    unit = attended * lax.rsqrt(jnp.mean(attended * attended, axis=0, keepdims=True) + unit_eps)
    gate = 1.0 / (1.0 + jnp.exp(-gate_ref[...]))
    out_ref[...] = (unit + gate * read_ref[...]).astype(bf16)


def merge(near, far, gate, read):
    cols, tokens = gate.shape
    heads = cols // HD
    flat_spec = pl.BlockSpec((HD, tokens), lambda h: (h, 0))

    def head_spec(*block):
        return pl.BlockSpec((1,) + block, lambda h: (h, 0, 0))

    return pl.pallas_call(
        functools.partial(merge_kernel, len(near), len(far)),
        out_shape=jax.ShapeDtypeStruct((cols, tokens), bf16),
        grid=(heads,),
        in_specs=[head_spec(HD, tokens), head_spec(1, tokens)] * len(near)
        + [head_spec(HD + TAIL, tokens)] * len(far)
        + [flat_spec] * 2,
        out_specs=flat_spec,
        compiler_params=pltpu.CompilerParams(vmem_limit_bytes=32 * 2**20),
        cost_estimate=pl.CostEstimate(
            flops=10 * (len(near) + len(far)) * cols * tokens,
            bytes_accessed=(4 * len(near) + 2 * len(far) + 10) * cols * tokens,
            transcendentals=cols * tokens,
        ),
    )(*(value for pair in near for value in pair), *far, gate, read)


def shards(
    tokens,
    gain,
    projection_weight,
    output_weight,
    persist,
    cache_page_slots,
    cached_length,
    page_keeper,
    page_slot_index,
    memory_state,
    retention,
    momentum,
    memory_step_scale,
    halving_updates,
):
    shard_tokens = tokens.shape[1]
    width = tokens.shape[2]
    cols = projection_weight.shape[2]
    devices = cache_page_slots.shape[1]
    span = cache_page_slots.shape[2]
    lanes = span // PAGE
    max_pages = page_keeper.shape[1]
    planes = devices // GROUP
    n_head = lax.axis_size("head")
    here = lax.axis_index("req")
    plane, place = here // GROUP, here % GROUP
    side = lax.axis_index("head")

    def swap(value, step):
        return lax.ppermute(value, "req", [(i, i ^ step) for i in range(devices)])

    def turn(value, step):
        return lax.ppermute(
            value, "head", [(i, (i - step) % n_head) for i in range(n_head)]
        )

    def projection(rows, weight):
        return dot(weight, rows, ((0,), (1,)))

    def norm(rows):
        x = rows.astype(f32)
        return (
            x * lax.rsqrt(jnp.mean(x * x, axis=-1, keepdims=True) + norm_eps) * gain.astype(f32)
        ).astype(bf16)

    def ordered(value, *earlier):
        return lax.optimization_barrier((value,) + earlier)[0]

    others = [turn(tokens[0], step) for step in range(1, n_head)]
    count = n_head * shard_tokens

    def rolled(value, shift):
        return lax.dynamic_slice_in_dim(
            jnp.concatenate([value, value], axis=1), shift * shard_tokens, count, 1
        )

    page_ids = jnp.arange(max_pages, dtype=jnp.int32)
    filled = jnp.clip(cached_length[0] - page_ids * PAGE, 0, PAGE)
    slot_of = page_keeper[0] * lanes + page_slot_index[0]
    keeper = (plane ^ jnp.arange(planes, dtype=jnp.int32))[:, None] * GROUP + (
        place ^ jnp.arange(GROUP, dtype=jnp.int32)
    )
    slot_ids = keeper[:, :, None] * lanes + jnp.arange(lanes, dtype=jnp.int32)
    slot_fill = jnp.sum(
        jnp.where(slot_of == slot_ids[..., None], filled, 0), axis=-1
    )

    offsets = list(range(2, planes)) + [1, 0]
    core = place % 2
    cache = cache_page_slots[0]
    by_plane = cache.reshape(planes, GROUP, span, 2, cols)

    def pair_of(d, after):
        start = (plane ^ d) * GROUP + ((place // 2) ^ 1) * 2
        return as_it_lies(lax.dynamic_slice_in_dim(ordered(cache, after), start, 2, 0))

    def column_of(k, after):
        column = lax.dynamic_index_in_dim(ordered(by_plane, after), place ^ k, 1, keepdims=False)
        return as_it_lies(column)

    def relay(piece):
        return jnp.swapaxes(as_it_lies(piece), -3, -2)

    def with_fill(value, d):
        rows = jnp.concatenate([slot_fill[d], slot_fill[d ^ 1]], axis=0)
        rows = jnp.pad(rows, ((0, TAIL - 2 * GROUP), (0, value.shape[1] - lanes)))
        return jnp.concatenate([value, rows.astype(bf16)], axis=0)

    across, sibling, far_here, far_rest = {}, {}, {}, {}

    def pass_on(d, *earlier):
        piece = lax.dynamic_index_in_dim(ordered(across[d], *earlier), 1 - core, 0, keepdims=False)
        sibling[d] = swap(as_it_lies(piece), 1)

    first = offsets[0]
    piece = pair_of(first, gain)
    across[first] = swap(piece, 2)
    flat = ordered(projection_weight, piece).reshape(width, 4 * cols)
    normed_here = norm(tokens[0])
    query_here = projection(normed_here, flat[:, :cols]).astype(bf16)
    if first:
        far_here[first] = swap(with_fill(query_here, first), first * GROUP)
    if len(offsets) > 1:
        piece = pair_of(offsets[1], query_here)
        across[offsets[1]] = swap(piece, 2)
    normed_rest = norm(ordered(jnp.concatenate(others, axis=0), piece))
    query_rest = projection(normed_rest, flat[:, :cols]).astype(bf16)
    if first:
        far_rest[first] = swap(query_rest, first * GROUP)
    beside = swap(column_of(1, query_rest), 1)
    projected = projection(
        jnp.concatenate([normed_here, normed_rest], axis=0), ordered(flat, query_rest)[:, cols:]
    )
    queries = jnp.concatenate([query_here, query_rest], axis=1)
    own_keys = projected[:cols].astype(bf16)
    own_values = projected[cols : 2 * cols].astype(bf16)
    gate = projected[2 * cols :]

    pass_on(first, projected)
    att, lse = own_attention(side, shard_tokens, queries, own_keys, own_values, persist)
    near, far = [(att, lse)], []
    near_kv = relay(column_of(0, lse))
    beside_kv = relay(ordered(beside, lse))
    done = beside_kv
    for i, d in enumerate(offsets):
        if i:
            pass_on(d, done)
        if d and d % 2 == 0:
            if d != first:
                far_here[d] = swap(with_fill(ordered(query_here, done), d), d * GROUP)
                far_rest[d] = swap(ordered(query_rest, done), d * GROUP)
            far_here[d ^ 1] = swap(ordered(far_here[d], done), GROUP)
            far_rest[d ^ 1] = swap(ordered(far_rest[d], done), GROUP)
        if i + 2 < len(offsets):
            across[offsets[i + 2]] = swap(pair_of(offsets[i + 2], across[d]), 2)
        if i == len(offsets) - 3:
            far_here[1] = swap(with_fill(ordered(queries, sibling[d]), 1), GROUP)
        far_kv = relay(lax.dynamic_index_in_dim(across[d], core, 0))
        kvs = [near_kv, beside_kv, far_kv, relay(sibling[d])[None]]
        at = [plane ^ d, plane ^ d, jnp.zeros_like(core), jnp.zeros_like(core)]
        if d:
            rows = cols + GROUP * (d % 2 if d > 1 else 0)
            halves = [far_here[d], far_rest[d]] if d > 1 else [far_here[d]]
            if d > 1 and shard_tokens % HD:
                halves = [jnp.concatenate([far_here[d][:cols], far_rest[d]], axis=1)]
            fill = far_here[d][rows : rows + GROUP, :lanes].astype(jnp.int32)
            (done,) = cache_attention(fill, halves, kvs, at, True, done)
            far.append(swap(done, d * GROUP))
        else:
            for part in (slice(0, 3), slice(3, 4)):
                pair = cache_attention(slot_fill[0, part], [queries], kvs[part], at[part], False, done)
                near.append(pair)
                done = pair[1]
        if i == 0:
            read, new_state = memory_pass(
                retention, momentum, memory_step_scale, halving_updates,
                *(
                    rolled(ordered(value, done), (n_head - side) % n_head)
                    for value in (queries, own_keys, own_values)
                ),
                memory_state[:, 0],
            )
            memory_read = rolled(read, side)
            done = read
        if i == 1:
            late = done
    head_out = merge(near, far, gate, memory_read)

    layer = jnp.zeros((shard_tokens, width), f32)
    for step in range(n_head):
        away = (n_head - step) % n_head
        part = head_out[:, away * shard_tokens : (away + 1) * shard_tokens]
        weight = output_weight
        if step:
            part = turn(part, step)
            weight = turn(ordered(output_weight, late), step)
        layer = layer + dot(part, weight, ((0,), (0,))).astype(bf16).astype(f32)
    return (layer.astype(bf16)[None], new_state[:, None])


def solution(mesh):
    in_specs = (
        P("req", "head", None),
        P(),
        P(None, None, "head"),
        P("head", None),
        P(None, None, "head"),
        P("req", None, None, None, "head"),
        P("req"),
        P("req", None),
        P("req", None),
        P(None, "req", "head", None, None),
        P("req", "head"),
        P("req", "head"),
        P("req", "head"),
        P("req", None),
    )
    out_specs = (P("req", "head", None), P(None, "req", "head", None, None))
    return jax.shard_map(shards, mesh=mesh, in_specs=in_specs, out_specs=out_specs, check_vma=False)
```

```python
import functools
import math

import jax
import jax.numpy as jnp
from jax import lax
from jax.experimental import pallas as pl
from jax.experimental.pallas import tpu as pltpu
from jax.sharding import PartitionSpec as P

HD = 128
BLK = 64
PAGE = 32
GROUP = 4


norm_eps = 1e-05
unit_eps = 1e-06
LOG2E = math.log2(math.e)
MASKED = -1e30
LAST = pl.CostEstimate(flops=6 * 10**9, bytes_accessed=1, transcendentals=0)
VMEM_LIMIT = 32 * 2**20
TAIL = 16
f32 = jnp.float32
bf16 = jnp.bfloat16
COST = pl.CostEstimate(flops=1, bytes_accessed=1, transcendentals=0)


def dot(left, right, contract=((1,), (0,)), precision=None):
    return lax.dot_general(
        left, right, (contract, ((), ())), precision=precision, preferred_element_type=f32
    )


def deal_kernel(counts, at_ref, from_ref, after_ref, *refs):
    del after_ref
    outs, (held, into, out_of) = refs[: len(counts)], refs[len(counts) :]
    places = [(out, i) for count, out in zip(counts, outs) for i in range(count)]
    reads, writes = [], []
    for at, (out, i) in enumerate(places):
        reads.append(pltpu.make_async_copy(from_ref.at[at_ref[at]], held.at[at], into.at[at]))
        writes.append(pltpu.make_async_copy(held.at[at], out.at[i], out_of.at[at]))
    for copy in reads:
        copy.start()
    for read, write in zip(reads, writes):
        read.wait()
        write.start()
    for copy in writes:
        copy.wait()


def deal(source, hands, after):
    counts = [len(rows) for rows in hands]
    total = sum(counts)
    anywhere = pl.BlockSpec(memory_space=pl.ANY)
    return pl.pallas_call(
        functools.partial(deal_kernel, counts),
        out_shape=[
            jax.ShapeDtypeStruct((count,) + source.shape[1:], source.dtype) for count in counts
        ],
        grid_spec=pltpu.PrefetchScalarGridSpec(
            num_scalar_prefetch=1,
            in_specs=[anywhere] * 2,
            out_specs=[anywhere] * len(counts),
            scratch_shapes=[
                pltpu.VMEM((total,) + source.shape[1:], source.dtype),
                pltpu.SemaphoreType.DMA((total,)),
                pltpu.SemaphoreType.DMA((total,)),
            ],
        ),
        compiler_params=pltpu.CompilerParams(vmem_limit_bytes=56 * 2**20),
        cost_estimate=COST,
    )(jnp.stack([row for rows in hands for row in rows]), source, after)


def cache_kernel(shape, sent, at_ref, after_ref, q_ref, fill_ref, *refs):
    del after_ref
    span, heads, count, fill_row = shape
    kv_refs = refs[:count]
    outs = refs[count:-6]
    kept_ref, wide_ref, bias_ref, score_ref, tail_ref, sems = refs[-6:]
    scale = LOG2E / math.sqrt(HD)
    head = pl.program_id(0)

    @pl.when(head == 0)
    def _():
        copies = [
            pltpu.make_async_copy(kv_refs[g].at[at_ref[g]], kept_ref.at[g], sems.at[g])
            for g in range(count)
        ]
        for copy in copies:
            copy.start()
        row = lax.broadcasted_iota(jnp.int32, (span, HD), 0)
        lane = lax.broadcasted_iota(jnp.int32, (span, HD), 1)
        slot = jnp.where(row // PAGE == lane, 1.0, 0.0).astype(bf16)
        filled = dot(slot, fill_ref[...], ((1,), (1,)))
        row_f = (row % PAGE).astype(f32)
        tail_ref[...] = jnp.zeros_like(tail_ref)
        for g in range(count):
            column = filled[:, fill_row + g : fill_row + g + 1]
            bias_ref[pl.ds(g * span, span), :] = jnp.where(row_f < column, 0.0, MASKED)
            copies[g].wait()
            wide_ref[g] = kept_ref[g].astype(f32)

    def part_of(g, which):
        rows = pl.ds(2 * head + which, span, stride=2 * heads)
        return wide_ref[g, rows, :].astype(bf16)

    q = q_ref[...]
    tokens = q.shape[1]
    top = jnp.full((1, tokens), MASKED, f32)
    for g in range(count):
        rows = pl.ds(g * span, span)
        score = dot(part_of(g, 0), q) * scale + jnp.tile(bias_ref[rows, :], (1, tokens // HD))
        score_ref[rows, :] = score
        top = jnp.maximum(top, jnp.max(score, axis=0, keepdims=True))
    total = jnp.zeros((1, tokens), f32)
    mixed = jnp.zeros((HD, tokens), f32)
    for g in range(count):
        rows = pl.ds(g * span, span)
        weight = jnp.exp2(score_ref[rows, :] - top)
        total = total + jnp.sum(weight, axis=0, keepdims=True)
        mixed = mixed + dot(part_of(g, 1), weight.astype(bf16), ((0,), (0,)))
    attended = mixed / total
    lse = top + jnp.log2(total)
    if sent:
        (out,) = outs
        rows = pl.ds(pl.multiple_of(head * HD, HD), HD)
        out[rows, :] = attended.astype(bf16)
        high = lse.astype(bf16).astype(f32)
        middle = (lse - high).astype(bf16).astype(f32)
        for i, term in enumerate((high, middle, lse - high - middle)):
            tail_ref[pl.ds(i * heads + head, 1), :] = term

        @pl.when(head == heads - 1)
        def _():
            out[pl.ds(heads * HD, TAIL), :] = tail_ref[...].astype(bf16)
    else:
        outs[0][0] = attended
        outs[1][0] = lse


def cache_attention(queries, cols, fill, fill_row, kvs, at, sent, after, cost=COST):
    count = len(kvs)
    heads = cols // HD
    span = kvs[0].shape[1] // (2 * heads)
    tokens = queries.shape[1]
    fill_at = cols // TAIL if fill.shape[0] > TAIL else 0

    def head_spec(*block):
        return pl.BlockSpec((1,) + block, lambda h, at: (h, 0, 0))

    if sent:
        out_shape = (jax.ShapeDtypeStruct((cols + TAIL, tokens), bf16),)
        out_specs = (pl.BlockSpec((cols + TAIL, tokens), lambda h, at: (0, 0)),)
    else:
        out_shape = (
            jax.ShapeDtypeStruct((heads, HD, tokens), f32),
            jax.ShapeDtypeStruct((heads, 1, tokens), f32),
        )
        out_specs = (head_spec(HD, tokens), head_spec(1, tokens))
    return pl.pallas_call(
        functools.partial(cache_kernel, (span, heads, count, fill_row), sent),
        out_shape=out_shape,
        grid_spec=pltpu.PrefetchScalarGridSpec(
            num_scalar_prefetch=1,
            grid=(heads,),
            in_specs=[
                pl.BlockSpec(memory_space=pl.ANY),
                pl.BlockSpec((HD, tokens), lambda h, at: (h, 0)),
                pl.BlockSpec((TAIL, HD), lambda h, at: (fill_at, 0)),
            ]
            + [pl.BlockSpec(memory_space=pl.ANY)] * count,
            out_specs=out_specs,
            scratch_shapes=[
                pltpu.VMEM((count,) + kvs[0].shape[1:], bf16),
                pltpu.VMEM((count,) + kvs[0].shape[1:], f32),
                pltpu.VMEM((count * span, HD), f32),
                pltpu.VMEM((count * span, tokens), f32),
                pltpu.VMEM((TAIL, tokens), f32),
                pltpu.SemaphoreType.DMA((count,)),
            ],
        ),
        compiler_params=pltpu.CompilerParams(vmem_limit_bytes=VMEM_LIMIT),
        cost_estimate=cost,
    )(jnp.stack(at), after, queries, fill, *kvs)


def own_kernel(shard, shards_in_all, side_ref, q_ref, k_ref, v_ref, persist_ref, att_ref, lse_ref):
    def place(axis):
        at = lax.broadcasted_iota(jnp.int32, (tokens, tokens), axis)
        return lax.rem(side_ref[0] + at // shard, shards_in_all) * shard + lax.rem(at, shard)

    scale = LOG2E / math.sqrt(HD)
    q = q_ref[...]
    tokens = q.shape[1]
    score_p = dot(persist_ref[0], q) * scale
    score_t = dot(k_ref[...].T, q) * scale
    score_t = jnp.where(place(0) <= place(1), score_t, MASKED)
    top = jnp.maximum(
        jnp.max(score_p, axis=0, keepdims=True), jnp.max(score_t, axis=0, keepdims=True)
    )
    weight_p = jnp.exp2(score_p - top)
    weight_t = jnp.exp2(score_t - top)
    total = jnp.sum(weight_p, axis=0, keepdims=True) + jnp.sum(weight_t, axis=0, keepdims=True)
    mixed = dot(v_ref[...], weight_t.astype(bf16)) + dot(
        persist_ref[1], weight_p.astype(bf16), ((0,), (0,))
    )
    att_ref[0] = mixed / total
    lse_ref[0] = top + jnp.log2(total)


def own_attention(side, shard, q, k, v, persist):
    cols, tokens = q.shape
    heads = cols // HD
    head_spec = pl.BlockSpec((HD, tokens), lambda h: (h, 0))
    return pl.pallas_call(
        functools.partial(own_kernel, shard, tokens // shard),
        out_shape=(
            jax.ShapeDtypeStruct((heads, HD, tokens), f32),
            jax.ShapeDtypeStruct((heads, 1, tokens), f32),
        ),
        grid=(heads,),
        in_specs=[pl.BlockSpec(memory_space=pltpu.SMEM)]
        + [head_spec] * 3
        + [pl.BlockSpec((2, persist.shape[1], HD), lambda h: (0, 0, h))],
        out_specs=(
            pl.BlockSpec((1, HD, tokens), lambda h: (h, 0, 0)),
            pl.BlockSpec((1, 1, tokens), lambda h: (h, 0, 0)),
        ),
        compiler_params=pltpu.CompilerParams(vmem_limit_bytes=VMEM_LIMIT),
        cost_estimate=COST,
    )(side[None], q, k, v, persist)


def memory_kernel(
    shards_in_all, side_ref, retention_ref, momentum_ref, step_ref, halving_ref, after_ref,
    q_ref, k_ref, v_ref, state_ref, read_ref, new_ref, kn_ref,
):
    del after_ref
    heads = state_ref.shape[1]
    tokens = q_ref.shape[1]
    shard = tokens // shards_in_all
    exact = lax.Precision.HIGHEST
    ms = [state_ref[0, h] for h in range(heads)]
    ss = [state_ref[1, h] for h in range(heads)]
    for a in range(shards_in_all):
        start = lax.rem(a + shards_in_all - side_ref[0], shards_in_all) * shard
        lanes = slice(None) if shards_in_all == 1 else pl.ds(pl.multiple_of(start, HD), shard)
        units = []
        for h in range(heads):
            rows = pl.ds(h * HD, HD)
            q = q_ref[rows, lanes].astype(f32)
            k = k_ref[rows, lanes].astype(f32)
            qn = q * lax.rsqrt(jnp.sum(q * q, axis=0, keepdims=True) + unit_eps)
            kn = k * lax.rsqrt(jnp.sum(k * k, axis=0, keepdims=True) + unit_eps)
            kn_ref[h] = kn.T
            units.append((qn, kn, v_ref[rows, lanes].astype(f32), []))
        for b in range(shard // BLK):
            lower, upper = b * BLK, (b + 1) * BLK
            for h in range(heads):
                qn, kn, values, reads = units[h]
                both = jnp.concatenate([kn[:, lower:upper], qn[:, lower:upper]], axis=1)
                product = dot(ms[h], both, precision=exact)
                error = product[:, :BLK] - values[:, lower:upper]
                reads.append(product[:, BLK:])
                grad = dot(error, kn_ref[h, lower:upper, :], precision=exact)
                ss[h] = momentum_ref[0, h] * ss[h] - step_ref[0, h] * grad
                halving = halving_ref[0, a * (shard // BLK) + b]
                keep = retention_ref[0, h] * jnp.where(halving == 1, 0.5, 1.0)
                ms[h] = keep * ms[h] + ss[h]
        for h in range(heads):
            read_ref[pl.ds(h * HD, HD), lanes] = jnp.concatenate(units[h][3], axis=1)
    for h in range(heads):
        new_ref[0, h] = ms[h]
        new_ref[1, h] = ss[h]


def memory_pass(side, shard, retention, momentum, step, halving, after, q, k, v, state):
    cols, tokens = q.shape
    heads = cols // HD
    count = tokens // shard if shard % HD == 0 else 1

    def rolled(value, shift):
        twice = jnp.concatenate([value, value], axis=1)
        return lax.dynamic_slice_in_dim(twice, shift * shard, tokens, 1)

    if count == 1:
        back = (tokens // shard - side) % (tokens // shard)
        q, k, v = rolled(q, back), rolled(k, back), rolled(v, back)
    smem = pl.BlockSpec(memory_space=pltpu.SMEM)
    vmem = pl.BlockSpec(memory_space=pltpu.VMEM)
    read, new = pl.pallas_call(
        functools.partial(memory_kernel, count),
        out_shape=(
            jax.ShapeDtypeStruct((cols, tokens), f32),
            jax.ShapeDtypeStruct(state.shape, f32),
        ),
        in_specs=[smem] * 5 + [pl.BlockSpec(memory_space=pl.ANY)] + [vmem] * 4,
        out_specs=(vmem, vmem),
        scratch_shapes=[pltpu.VMEM((heads, tokens // count, HD), f32)],
        compiler_params=pltpu.CompilerParams(vmem_limit_bytes=VMEM_LIMIT),
        cost_estimate=COST,
    )(side[None], retention, momentum, step, halving, after, q, k, v, state)
    return (read if count > 1 else rolled(read, side)), new


def merge_kernel(near, heads, *refs):
    pairs = [(refs[2 * i][0], refs[2 * i + 1][0]) for i in range(near)]
    for att, tail in zip(refs[2 * near : -3 : 2], refs[2 * near + 1 : -3 : 2]):
        row = lax.broadcasted_iota(jnp.int32, tail.shape, 0)
        mine = (lax.rem(row, heads) == pl.program_id(0)) & (row < 3 * heads)
        lse = jnp.sum(jnp.where(mine, tail[...].astype(f32), 0.0), axis=0, keepdims=True)
        pairs.append((att[...].astype(f32), lse))
    gate_ref, read_ref, out_ref = refs[-3:]
    top = functools.reduce(jnp.maximum, [lse for _, lse in pairs])
    total = jnp.zeros_like(top)
    mixed = jnp.zeros(out_ref.shape, f32)
    for att, lse in pairs:
        share = jnp.exp2(lse - top)
        total = total + share
        mixed = mixed + att * share
    attended = mixed / total
    unit = attended * lax.rsqrt(jnp.mean(attended * attended, axis=0, keepdims=True) + unit_eps)
    gate = 1.0 / (1.0 + jnp.exp(-gate_ref[...]))
    out_ref[...] = (unit + gate * read_ref[...]).astype(bf16)


def merge(near, far, projected, read):
    cols, tokens = read.shape
    heads = cols // HD
    gates = projected.shape[0] // HD - heads
    flat_spec = pl.BlockSpec((HD, tokens), lambda h: (h, 0))

    def head_spec(*block):
        return pl.BlockSpec((1,) + block, lambda h: (h, 0, 0))

    return pl.pallas_call(
        functools.partial(merge_kernel, len(near), heads),
        out_shape=jax.ShapeDtypeStruct((cols, tokens), bf16),
        grid=(heads,),
        in_specs=[head_spec(HD, tokens), head_spec(1, tokens)] * len(near)
        + [flat_spec, pl.BlockSpec((TAIL, tokens), lambda h: (cols // TAIL, 0))] * len(far)
        + [pl.BlockSpec((HD, tokens), lambda h: (gates + h, 0)), flat_spec],
        out_specs=flat_spec,
        compiler_params=pltpu.CompilerParams(vmem_limit_bytes=VMEM_LIMIT),
        cost_estimate=pl.CostEstimate(
            flops=10 * (len(near) + len(far)) * cols * tokens,
            bytes_accessed=(4 * len(near) + 2 * len(far) + 10) * cols * tokens,
            transcendentals=cols * tokens,
        ),
    )(*(value for pair in near for value in pair), *(f for f in far for _ in (0, 1)), projected, read)


def shards(
    tokens,
    gain,
    projection_weight,
    output_weight,
    persist,
    cache_page_slots,
    cached_length,
    page_keeper,
    page_slot_index,
    memory_state,
    retention,
    momentum,
    memory_step_scale,
    halving_updates,
):
    shard_tokens = tokens.shape[1]
    width = tokens.shape[2]
    cols = projection_weight.shape[2]
    devices = cache_page_slots.shape[1]
    span = cache_page_slots.shape[2]
    lanes = span // PAGE
    max_pages = page_keeper.shape[1]
    planes = devices // GROUP
    n_head = lax.axis_size("head")
    here = lax.axis_index("req")
    plane, place = here // GROUP, here % GROUP
    side = lax.axis_index("head")

    def swap(value, step):
        return lax.ppermute(value, "req", [(i, i ^ step) for i in range(devices)])

    def turn(value, step):
        return lax.ppermute(
            value, "head", [(i, (i - step) % n_head) for i in range(n_head)]
        )

    def projection(rows, weight):
        return dot(weight, rows, ((0,), (1,)))

    def norm(rows):
        x = rows.astype(f32)
        return (
            x * lax.rsqrt(jnp.mean(x * x, axis=-1, keepdims=True) + norm_eps) * gain.astype(f32)
        ).astype(bf16)

    def ordered(value, *earlier):
        return lax.optimization_barrier((value,) + earlier)[0]

    others = [turn(tokens[0], step) for step in range(1, n_head)]

    page_ids = jnp.arange(max_pages, dtype=jnp.int32)
    filled = jnp.clip(cached_length[0] - page_ids * PAGE, 0, PAGE)
    slot_of = page_keeper[0] * lanes + page_slot_index[0]
    keeper = (plane ^ jnp.arange(planes, dtype=jnp.int32))[:, None] * GROUP + (
        place ^ jnp.arange(GROUP, dtype=jnp.int32)
    )
    slot_ids = keeper[:, :, None] * lanes + jnp.arange(lanes, dtype=jnp.int32)
    slot_fill = jnp.sum(
        jnp.where(slot_of == slot_ids[..., None], filled, 0), axis=-1
    )

    offsets = list(range(2, planes)) + [1, 0]
    core = place % 2
    cache = cache_page_slots[0]
    heads = cols // HD
    cache = cache.reshape(devices, span, 2, heads, HD).transpose(0, 1, 3, 2, 4)
    cache = cache.reshape(devices, span * heads * 2, HD)

    hands = []
    for d in offsets:
        start = (plane ^ d) * GROUP + ((place // 2) ^ 1) * 2
        hands.append([start, start + 1])
    for k in (1, 0):
        hands.append([z * GROUP + (place ^ k) for z in range(planes)])
    pieces = dict(zip(offsets, deal(cache, hands[:1], gain)))

    def with_fill(value, d):
        rows = jnp.concatenate([slot_fill[d], slot_fill[d ^ 1]], axis=0)
        rows = jnp.pad(rows, ((0, TAIL - 2 * GROUP), (0, value.shape[1] - lanes)))
        return jnp.concatenate([value, rows.astype(bf16)], axis=0)

    across, sibling, far_here, far_rest = {}, {}, {}, {}

    def pass_on(d, *earlier):
        piece = ordered(across[d], *earlier)
        sibling[d] = swap(lax.dynamic_index_in_dim(piece, 1 - core, 0), 1)

    first, second = offsets[:2]
    across[first] = swap(pieces[first], 2)
    flat = ordered(projection_weight, pieces[first]).reshape(width, 4 * cols)
    normed_here = norm(tokens[0])
    query_here = projection(normed_here, flat[:, :cols]).astype(bf16)
    far_here[first] = swap(with_fill(query_here, first), first * GROUP)
    far_here[1] = swap(with_fill(query_here, 1), GROUP)
    *rest, column, own = deal(cache, hands[1:], query_here)
    pieces |= zip(offsets[1:], rest)
    beside = swap(ordered(column, far_here[1]), 1)
    across[second] = swap(pieces[second], 2)
    normed_rest = norm(ordered(jnp.concatenate(others, axis=0), query_here))
    query_rest = projection(normed_rest, flat[:, :cols]).astype(bf16)
    far_rest[first] = swap(query_rest, first * GROUP)
    projected = projection(
        jnp.concatenate([normed_here, normed_rest], axis=0), ordered(flat, query_rest)[:, cols:]
    )
    queries = jnp.concatenate([query_here, query_rest], axis=1)
    own_keys = projected[:cols].astype(bf16)
    own_values = projected[cols : 2 * cols].astype(bf16)
    far_rest[1] = swap(ordered(query_rest, far_here[1], own_values), GROUP)
    sent = [far_here[first], far_here[1], far_rest[first], far_rest[1]]

    att, lse = own_attention(side, shard_tokens, queries, own_keys, own_values, persist)
    near, far = [(att, lse)], []
    pass_on(first, lse, *sent)
    asked = {}
    done = lse
    fill_here = jnp.pad(slot_fill[0], ((0, TAIL - GROUP), (0, HD - lanes))).astype(bf16)
    for i, d in enumerate(offsets):
        if i and d:
            pass_on(d, att)
        if d == 1 or (d and d % 2 == 0):
            if d not in far_here:
                far_here[d] = swap(with_fill(ordered(query_here, done), d), d * GROUP)
                far_rest[d] = swap(ordered(query_rest, done), d * GROUP)
            here_rows = jnp.pad(ordered(far_here[d], *sent), ((0, TAIL), (0, 0)))
            rest_rows = jnp.pad(ordered(far_rest[d], *sent), ((0, 2 * TAIL), (0, 0)))
            asked[d] = jnp.concatenate([here_rows, rest_rows], axis=1)
            if d > 1:
                asked[d ^ 1] = swap(asked[d], GROUP)
        if i + 2 < len(offsets):
            earlier = sent if i == 0 else [done]
            if i == 0:
                across[offsets[i + 2]] = swap(ordered(pieces[offsets[i + 2]], across[d], *earlier), 2)
        kvs = [own, beside, across[d], sibling.get(d)]
        at = [plane ^ d, plane ^ d, core, jnp.zeros_like(core)]
        if d:
            if d == 1:
                done = ordered(done, far[0])
            row = GROUP * (d % 2 if d > 1 else 0)
            (done,) = cache_attention(
                asked[d], cols, asked[d], row, kvs, at, True, done, LAST if d == 1 else COST
            )
            att = done
            far.append(swap(done, d * GROUP))
            if 0 < i < len(offsets) - 2:
                across[offsets[i + 2]] = swap(ordered(pieces[offsets[i + 2]], done), 2)
        else:
            for part in (slice(0, 2), slice(2, 3), slice(3, 4)):
                pair = cache_attention(
                    queries, cols, fill_here, part.start, kvs[part], at[part], False, done
                )
                near.append(pair)
                done = pair[1]
                if part.start == 0:
                    pass_on(d, done)
                    kvs[3] = sibling[d]
        if i == 0:
            memory_read, new_state = memory_pass(
                side, shard_tokens, retention, momentum, memory_step_scale, halving_updates,
                done, queries, own_keys, own_values, memory_state[:, 0],
            )
            done = memory_read
        if d == 1:
            late = across[d]
    head_out = merge(near, far, projected, memory_read)

    layer = jnp.zeros((shard_tokens, width), f32)
    for step in range(n_head):
        away = (n_head - step) % n_head
        part = head_out[:, away * shard_tokens : (away + 1) * shard_tokens]
        weight = output_weight
        if step:
            part = turn(part, step)
            weight = turn(ordered(output_weight, late), step)
        layer = layer + dot(part, weight, ((0,), (0,))).astype(bf16).astype(f32)
    return (layer.astype(bf16)[None], new_state[:, None])


def solution(mesh):
    in_specs = (
        P("req", "head", None),
        P(),
        P(None, None, "head"),
        P("head", None),
        P(None, None, "head"),
        P("req", None, None, None, "head"),
        P("req"),
        P("req", None),
        P("req", None),
        P(None, "req", "head", None, None),
        P("req", "head"),
        P("req", "head"),
        P("req", "head"),
        P("req", None),
    )
    out_specs = (P("req", "head", None), P(None, "req", "head", None, None))
    return jax.shard_map(shards, mesh=mesh, in_specs=in_specs, out_specs=out_specs, check_vma=False)
```

```python
import functools
import math

import jax
import jax.numpy as jnp
from jax import lax
from jax.experimental import pallas as pl
from jax.experimental.pallas import tpu as pltpu
from jax.sharding import PartitionSpec as P

HD = 128
BLK = 64
PAGE = 32
GROUP = 4


norm_eps = 1e-05
unit_eps = 1e-06
LOG2E = math.log2(math.e)
MASKED = -1e30
LAST = pl.CostEstimate(flops=6 * 10**9, bytes_accessed=1, transcendentals=0)
VMEM_LIMIT = 16 * 2**20
TAIL = 16
f32 = jnp.float32
bf16 = jnp.bfloat16
COST = pl.CostEstimate(flops=1, bytes_accessed=1, transcendentals=0)


def dot(left, right, contract=((1,), (0,)), precision=None):
    return lax.dot_general(
        left, right, (contract, ((), ())), precision=precision, preferred_element_type=f32
    )


def fence_kernel(*refs):
    refs[-1][...] = jnp.zeros_like(refs[-1])


def fence(*earlier):
    return pl.pallas_call(
        fence_kernel,
        out_shape=jax.ShapeDtypeStruct((8, HD), f32),
        in_specs=[pl.BlockSpec(memory_space=pl.ANY)] * len(earlier),
        compiler_params=pltpu.CompilerParams(vmem_limit_bytes=2**20),
        cost_estimate=LAST,
    )(*earlier)


def deal_kernel(counts, at_ref, from_ref, after_ref, *refs):
    del after_ref
    outs, (held, into, out_of) = refs[: len(counts)], refs[len(counts) :]
    places = [(out, i) for count, out in zip(counts, outs) for i in range(count)]
    reads, writes = [], []
    for at, (out, i) in enumerate(places):
        reads.append(pltpu.make_async_copy(from_ref.at[at_ref[at]], held.at[at], into.at[at]))
        writes.append(pltpu.make_async_copy(held.at[at], out.at[i], out_of.at[at]))
    for copy in reads:
        copy.start()
    for read, write in zip(reads, writes):
        read.wait()
        write.start()
    for copy in writes:
        copy.wait()


def deal(source, hands, after, vmem_limit):
    counts = [len(rows) for rows in hands]
    total = sum(counts)
    anywhere = pl.BlockSpec(memory_space=pl.ANY)
    return pl.pallas_call(
        functools.partial(deal_kernel, counts),
        out_shape=[
            jax.ShapeDtypeStruct((count,) + source.shape[1:], source.dtype) for count in counts
        ],
        grid_spec=pltpu.PrefetchScalarGridSpec(
            num_scalar_prefetch=1,
            in_specs=[anywhere] * 2,
            out_specs=[anywhere] * len(counts),
            scratch_shapes=[
                pltpu.VMEM((total,) + source.shape[1:], source.dtype),
                pltpu.SemaphoreType.DMA((total,)),
                pltpu.SemaphoreType.DMA((total,)),
            ],
        ),
        compiler_params=pltpu.CompilerParams(vmem_limit_bytes=vmem_limit),
        cost_estimate=COST,
    )(jnp.stack([row for rows in hands for row in rows]), source, after)


def cache_kernel(shape, sent, at_ref, after_ref, q_ref, fill_ref, *refs):
    del after_ref
    span, heads, count, fill_row = shape
    kv_refs = refs[:count]
    outs = refs[count:-6]
    kept_ref, wide_ref, bias_ref, score_ref, tail_ref, sems = refs[-6:]
    scale = LOG2E / math.sqrt(HD)
    head = pl.program_id(0)

    @pl.when(head == 0)
    def _():
        copies = [
            pltpu.make_async_copy(kv_refs[g].at[at_ref[g]], kept_ref.at[g], sems.at[g])
            for g in range(count)
        ]
        for copy in copies:
            copy.start()
        row = lax.broadcasted_iota(jnp.int32, (span, HD), 0)
        lane = lax.broadcasted_iota(jnp.int32, (span, HD), 1)
        slot = jnp.where(row // PAGE == lane, 1.0, 0.0).astype(bf16)
        filled = dot(slot, fill_ref[...], ((1,), (1,)))
        row_f = (row % PAGE).astype(f32)
        tail_ref[...] = jnp.zeros_like(tail_ref)
        for g in range(count):
            column = filled[:, fill_row + g : fill_row + g + 1]
            bias_ref[pl.ds(g * span, span), :] = jnp.where(row_f < column, 0.0, MASKED)
            copies[g].wait()
            wide_ref[g] = kept_ref[g].astype(f32)

    def part_of(g, which):
        rows = pl.ds(2 * head + which, span, stride=2 * heads)
        return wide_ref[g, rows, :].astype(bf16)

    q = q_ref[...]
    tokens = q.shape[1]
    top = jnp.full((1, tokens), MASKED, f32)
    for g in range(count):
        rows = pl.ds(g * span, span)
        score = dot(part_of(g, 0), q) * scale + jnp.tile(bias_ref[rows, :], (1, tokens // HD))
        score_ref[rows, :] = score
        top = jnp.maximum(top, jnp.max(score, axis=0, keepdims=True))
    total = jnp.zeros((1, tokens), f32)
    mixed = jnp.zeros((HD, tokens), f32)
    for g in range(count):
        rows = pl.ds(g * span, span)
        weight = jnp.exp2(score_ref[rows, :] - top)
        total = total + jnp.sum(weight, axis=0, keepdims=True)
        mixed = mixed + dot(part_of(g, 1), weight.astype(bf16), ((0,), (0,)))
    attended = mixed / total
    lse = top + jnp.log2(total)
    if sent:
        (out,) = outs
        rows = pl.ds(pl.multiple_of(head * HD, HD), HD)
        out[rows, :] = attended.astype(bf16)
        high = lse.astype(bf16).astype(f32)
        middle = (lse - high).astype(bf16).astype(f32)
        for i, term in enumerate((high, middle, lse - high - middle)):
            tail_ref[pl.ds(i * heads + head, 1), :] = term

        @pl.when(head == heads - 1)
        def _():
            out[pl.ds(heads * HD, TAIL), :] = tail_ref[...].astype(bf16)
    else:
        outs[0][0] = attended
        outs[1][0] = lse


def cache_attention(queries, cols, fill, fill_row, kvs, at, sent, after):
    count = len(kvs)
    heads = cols // HD
    span = kvs[0].shape[1] // (2 * heads)
    tokens = queries.shape[1]
    fill_at = cols // TAIL if fill.shape[0] > TAIL else 0

    def head_spec(*block):
        return pl.BlockSpec((1,) + block, lambda h, at: (h, 0, 0))

    if sent:
        out_shape = (jax.ShapeDtypeStruct((cols + TAIL, tokens), bf16),)
        out_specs = (pl.BlockSpec((cols + TAIL, tokens), lambda h, at: (0, 0)),)
    else:
        out_shape = (
            jax.ShapeDtypeStruct((heads, HD, tokens), f32),
            jax.ShapeDtypeStruct((heads, 1, tokens), f32),
        )
        out_specs = (head_spec(HD, tokens), head_spec(1, tokens))
    return pl.pallas_call(
        functools.partial(cache_kernel, (span, heads, count, fill_row), sent),
        out_shape=out_shape,
        grid_spec=pltpu.PrefetchScalarGridSpec(
            num_scalar_prefetch=1,
            grid=(heads,),
            in_specs=[
                pl.BlockSpec(memory_space=pl.ANY),
                pl.BlockSpec((HD, tokens), lambda h, at: (h, 0)),
                pl.BlockSpec((TAIL, HD), lambda h, at: (fill_at, 0)),
            ]
            + [pl.BlockSpec(memory_space=pl.ANY)] * count,
            out_specs=out_specs,
            scratch_shapes=[
                pltpu.VMEM((count,) + kvs[0].shape[1:], bf16),
                pltpu.VMEM((count,) + kvs[0].shape[1:], f32),
                pltpu.VMEM((count * span, HD), f32),
                pltpu.VMEM((count * span, tokens), f32),
                pltpu.VMEM((TAIL, tokens), f32),
                pltpu.SemaphoreType.DMA((count,)),
            ],
        ),
        compiler_params=pltpu.CompilerParams(vmem_limit_bytes=VMEM_LIMIT),
        cost_estimate=COST,
    )(jnp.stack(at), after, queries, fill, *kvs)


def own_kernel(shard, shards_in_all, side_ref, q_ref, k_ref, v_ref, persist_ref, att_ref, lse_ref):
    def place(axis):
        at = lax.broadcasted_iota(jnp.int32, (tokens, tokens), axis)
        return lax.rem(side_ref[0] + at // shard, shards_in_all) * shard + lax.rem(at, shard)

    scale = LOG2E / math.sqrt(HD)
    q = q_ref[...]
    tokens = q.shape[1]
    score_p = dot(persist_ref[0], q) * scale
    score_t = dot(k_ref[...].T, q) * scale
    score_t = jnp.where(place(0) <= place(1), score_t, MASKED)
    top = jnp.maximum(
        jnp.max(score_p, axis=0, keepdims=True), jnp.max(score_t, axis=0, keepdims=True)
    )
    weight_p = jnp.exp2(score_p - top)
    weight_t = jnp.exp2(score_t - top)
    total = jnp.sum(weight_p, axis=0, keepdims=True) + jnp.sum(weight_t, axis=0, keepdims=True)
    mixed = dot(v_ref[...], weight_t.astype(bf16)) + dot(
        persist_ref[1], weight_p.astype(bf16), ((0,), (0,))
    )
    att_ref[0] = mixed / total
    lse_ref[0] = top + jnp.log2(total)


def own_attention(side, shard, q, k, v, persist):
    cols, tokens = q.shape
    heads = cols // HD
    head_spec = pl.BlockSpec((HD, tokens), lambda h: (h, 0))
    return pl.pallas_call(
        functools.partial(own_kernel, shard, tokens // shard),
        out_shape=(
            jax.ShapeDtypeStruct((heads, HD, tokens), f32),
            jax.ShapeDtypeStruct((heads, 1, tokens), f32),
        ),
        grid=(heads,),
        in_specs=[pl.BlockSpec(memory_space=pltpu.SMEM)]
        + [head_spec] * 3
        + [pl.BlockSpec((2, persist.shape[1], HD), lambda h: (0, 0, h))],
        out_specs=(
            pl.BlockSpec((1, HD, tokens), lambda h: (h, 0, 0)),
            pl.BlockSpec((1, 1, tokens), lambda h: (h, 0, 0)),
        ),
        compiler_params=pltpu.CompilerParams(vmem_limit_bytes=VMEM_LIMIT),
        cost_estimate=COST,
    )(side[None], q, k, v, persist)


def memory_kernel(
    shards_in_all, side_ref, retention_ref, momentum_ref, step_ref, halving_ref, after_ref,
    q_ref, k_ref, v_ref, state_ref, read_ref, new_ref, kn_ref,
):
    del after_ref
    heads = state_ref.shape[1]
    tokens = q_ref.shape[1]
    shard = tokens // shards_in_all
    exact = lax.Precision.HIGHEST
    ms = [state_ref[0, h] for h in range(heads)]
    ss = [state_ref[1, h] for h in range(heads)]
    for a in range(shards_in_all):
        start = lax.rem(a + shards_in_all - side_ref[0], shards_in_all) * shard
        lanes = slice(None) if shards_in_all == 1 else pl.ds(pl.multiple_of(start, HD), shard)
        units = []
        for h in range(heads):
            rows = pl.ds(h * HD, HD)
            q = q_ref[rows, lanes].astype(f32)
            k = k_ref[rows, lanes].astype(f32)
            qn = q * lax.rsqrt(jnp.sum(q * q, axis=0, keepdims=True) + unit_eps)
            kn = k * lax.rsqrt(jnp.sum(k * k, axis=0, keepdims=True) + unit_eps)
            kn_ref[h] = kn.T
            units.append((qn, kn, v_ref[rows, lanes].astype(f32), []))
        for b in range(shard // BLK):
            lower, upper = b * BLK, (b + 1) * BLK
            for h in range(heads):
                qn, kn, values, reads = units[h]
                both = jnp.concatenate([kn[:, lower:upper], qn[:, lower:upper]], axis=1)
                product = dot(ms[h], both, precision=exact)
                error = product[:, :BLK] - values[:, lower:upper]
                reads.append(product[:, BLK:])
                grad = dot(error, kn_ref[h, lower:upper, :], precision=exact)
                ss[h] = momentum_ref[0, h] * ss[h] - step_ref[0, h] * grad
                halving = halving_ref[0, a * (shard // BLK) + b]
                keep = retention_ref[0, h] * jnp.where(halving == 1, 0.5, 1.0)
                ms[h] = keep * ms[h] + ss[h]
        for h in range(heads):
            read_ref[pl.ds(h * HD, HD), lanes] = jnp.concatenate(units[h][3], axis=1)
    for h in range(heads):
        new_ref[0, h] = ms[h]
        new_ref[1, h] = ss[h]


def memory_pass(side, shard, retention, momentum, step, halving, after, q, k, v, state):
    cols, tokens = q.shape
    heads = cols // HD
    count = tokens // shard if shard % HD == 0 else 1

    def rolled(value, shift):
        twice = jnp.concatenate([value, value], axis=1)
        return lax.dynamic_slice_in_dim(twice, shift * shard, tokens, 1)

    if count == 1:
        back = (tokens // shard - side) % (tokens // shard)
        q, k, v = rolled(q, back), rolled(k, back), rolled(v, back)
    smem = pl.BlockSpec(memory_space=pltpu.SMEM)
    vmem = pl.BlockSpec(memory_space=pltpu.VMEM)
    read, new = pl.pallas_call(
        functools.partial(memory_kernel, count),
        out_shape=(
            jax.ShapeDtypeStruct((cols, tokens), f32),
            jax.ShapeDtypeStruct(state.shape, f32),
        ),
        in_specs=[smem] * 5 + [pl.BlockSpec(memory_space=pl.ANY)] + [vmem] * 4,
        out_specs=(vmem, vmem),
        scratch_shapes=[pltpu.VMEM((heads, tokens // count, HD), f32)],
        compiler_params=pltpu.CompilerParams(vmem_limit_bytes=VMEM_LIMIT),
        cost_estimate=COST,
    )(side[None], retention, momentum, step, halving, after, q, k, v, state)
    return (read if count > 1 else rolled(read, side)), new


def merge_kernel(near, heads, *refs):
    pairs = [(refs[2 * i][0], refs[2 * i + 1][0]) for i in range(near)]
    for att, tail in zip(refs[2 * near : -3 : 2], refs[2 * near + 1 : -3 : 2]):
        row = lax.broadcasted_iota(jnp.int32, tail.shape, 0)
        mine = (lax.rem(row, heads) == pl.program_id(0)) & (row < 3 * heads)
        lse = jnp.sum(jnp.where(mine, tail[...].astype(f32), 0.0), axis=0, keepdims=True)
        pairs.append((att[...].astype(f32), lse))
    gate_ref, read_ref, out_ref = refs[-3:]
    top = functools.reduce(jnp.maximum, [lse for _, lse in pairs])
    total = jnp.zeros_like(top)
    mixed = jnp.zeros(out_ref.shape, f32)
    for att, lse in pairs:
        share = jnp.exp2(lse - top)
        total = total + share
        mixed = mixed + att * share
    attended = mixed / total
    unit = attended * lax.rsqrt(jnp.mean(attended * attended, axis=0, keepdims=True) + unit_eps)
    gate = 1.0 / (1.0 + jnp.exp(-gate_ref[...]))
    out_ref[...] = (unit + gate * read_ref[...]).astype(bf16)


def merge(near, far, projected, read):
    cols, tokens = read.shape
    heads = cols // HD
    gates = projected.shape[0] // HD - heads
    flat_spec = pl.BlockSpec((HD, tokens), lambda h: (h, 0))

    def head_spec(*block):
        return pl.BlockSpec((1,) + block, lambda h: (h, 0, 0))

    return pl.pallas_call(
        functools.partial(merge_kernel, len(near), heads),
        out_shape=jax.ShapeDtypeStruct((cols, tokens), bf16),
        grid=(heads,),
        in_specs=[head_spec(HD, tokens), head_spec(1, tokens)] * len(near)
        + [flat_spec, pl.BlockSpec((TAIL, tokens), lambda h: (cols // TAIL, 0))] * len(far)
        + [pl.BlockSpec((HD, tokens), lambda h: (gates + h, 0)), flat_spec],
        out_specs=flat_spec,
        compiler_params=pltpu.CompilerParams(vmem_limit_bytes=VMEM_LIMIT),
        cost_estimate=pl.CostEstimate(
            flops=10 * (len(near) + len(far)) * cols * tokens,
            bytes_accessed=(4 * len(near) + 2 * len(far) + 10) * cols * tokens,
            transcendentals=cols * tokens,
        ),
    )(*(value for pair in near for value in pair), *(f for f in far for _ in (0, 1)), projected, read)


def shards(
    tokens,
    gain,
    projection_weight,
    output_weight,
    persist,
    cache_page_slots,
    cached_length,
    page_keeper,
    page_slot_index,
    memory_state,
    retention,
    momentum,
    memory_step_scale,
    halving_updates,
):
    shard_tokens = tokens.shape[1]
    width = tokens.shape[2]
    cols = projection_weight.shape[2]
    devices = cache_page_slots.shape[1]
    span = cache_page_slots.shape[2]
    lanes = span // PAGE
    max_pages = page_keeper.shape[1]
    planes = devices // GROUP
    n_head = lax.axis_size("head")
    here = lax.axis_index("req")
    plane, place = here // GROUP, here % GROUP
    side = lax.axis_index("head")

    def swap(value, step):
        return lax.ppermute(value, "req", [(i, i ^ step) for i in range(devices)])

    def turn(value, step):
        return lax.ppermute(
            value, "head", [(i, (i - step) % n_head) for i in range(n_head)]
        )

    def projection(rows, weight):
        return dot(weight, rows, ((0,), (1,)))

    def norm(rows):
        x = rows.astype(f32)
        return (
            x * lax.rsqrt(jnp.mean(x * x, axis=-1, keepdims=True) + norm_eps) * gain.astype(f32)
        ).astype(bf16)

    def ordered(value, *earlier):
        return lax.optimization_barrier((value,) + earlier)[0]

    others = [turn(tokens[0], step) for step in range(1, n_head)]

    page_ids = jnp.arange(max_pages, dtype=jnp.int32)
    filled = jnp.clip(cached_length[0] - page_ids * PAGE, 0, PAGE)
    slot_of = page_keeper[0] * lanes + page_slot_index[0]
    keeper = (plane ^ jnp.arange(planes, dtype=jnp.int32))[:, None] * GROUP + (
        place ^ jnp.arange(GROUP, dtype=jnp.int32)
    )
    slot_ids = keeper[:, :, None] * lanes + jnp.arange(lanes, dtype=jnp.int32)
    slot_fill = jnp.sum(
        jnp.where(slot_of == slot_ids[..., None], filled, 0), axis=-1
    )

    offsets = list(range(2, planes)) + [1, 0]
    core = place % 2
    cache = cache_page_slots[0]
    heads = cols // HD
    cache = cache.reshape(devices, span, 2, heads, HD).transpose(0, 1, 3, 2, 4)
    cache = cache.reshape(devices, span * heads * 2, HD)

    hands = []
    for d in offsets:
        start = (plane ^ d) * GROUP + ((place // 2) ^ 1) * 2
        hands.append([start, start + 1])
    for k in (1, 0):
        hands.append([z * GROUP + (place ^ k) for z in range(planes)])
    *pieces, column, own = deal(cache, hands, gain, 56 * 2**20)
    pieces = dict(zip(offsets, pieces))

    def with_fill(value, d):
        rows = jnp.concatenate([slot_fill[d], slot_fill[d ^ 1]], axis=0)
        tail = TAIL if d == 1 else 2 * TAIL
        rows = jnp.pad(rows, ((0, tail - 2 * GROUP), (0, value.shape[1] - lanes)))
        return jnp.concatenate([value, rows.astype(bf16)], axis=0)

    across, sibling, far_here, far_rest = {}, {}, {}, {}

    def pass_on(d, *earlier):
        piece = ordered(across[d], *earlier)
        if d:
            (piece,) = deal(piece, [[1 - core]], gain, 2 * 2**20)
        else:
            piece = lax.dynamic_index_in_dim(piece, 1 - core, 0)
        sibling[d] = swap(piece, 1)

    first, second = offsets[:2]
    across[first] = swap(pieces[first], 2)
    flat = ordered(projection_weight, pieces[first]).reshape(width, 4 * cols)
    normed_here = norm(tokens[0])
    query_here = projection(normed_here, flat[:, :cols]).astype(bf16)
    far_here[first] = swap(with_fill(query_here, first), first * GROUP)
    far_here[1] = swap(with_fill(query_here, 1), GROUP)
    beside = swap(column, 1)
    normed_rest = norm(ordered(jnp.concatenate(others, axis=0), query_here))
    query_rest = projection(normed_rest, flat[:, :cols]).astype(bf16)
    far_rest[first] = swap(query_rest, first * GROUP)
    across[second] = swap(ordered(pieces[second], query_rest, beside), 2)
    projected = projection(
        jnp.concatenate([normed_here, normed_rest], axis=0), ordered(flat, query_rest)[:, cols:]
    )
    queries = jnp.concatenate([query_here, query_rest], axis=1)
    own_keys = projected[:cols].astype(bf16)
    own_values = projected[cols : 2 * cols].astype(bf16)
    far_rest[1] = swap(ordered(query_rest, far_here[1], own_values), GROUP)

    att, lse = own_attention(side, shard_tokens, queries, own_keys, own_values, persist)
    near, far = [(att, lse)], []
    fill_here = jnp.pad(slot_fill[0], ((0, TAIL - GROUP), (0, HD - lanes))).astype(bf16)
    pass_on(first, lse)

    def whole_of(d):
        rest_rows = ((0, far_here[d].shape[0] - cols), (0, 0))
        rest_rows = jnp.pad(far_rest[d], rest_rows)
        return jnp.concatenate([far_here[d], rest_rows], axis=1)

    asked = {}
    done = fence(lse)
    for i, d in enumerate(offsets):
        if i and d:
            pass_on(d, done)
        if d == 1:
            asked[1] = whole_of(1)
        if d and d % 2 == 0:
            if d not in far_here:
                far_here[d] = swap(with_fill(ordered(query_here, done), d), d * GROUP)
                far_rest[d] = swap(ordered(query_rest, done), d * GROUP)
            asked[d] = whole_of(d)
            asked[d ^ 1] = swap(asked[d], GROUP)
        if i + 2 < len(offsets):
            earlier = [across[d], far_here[d], far_rest[d]] if i == 0 else [done, far_rest[1]]
            across[offsets[i + 2]] = swap(ordered(pieces[offsets[i + 2]], *earlier), 2)
        kvs = [own, beside, across[d], sibling.get(d)]
        at = [plane ^ d, plane ^ d, core, jnp.zeros_like(core)]
        if d:
            if d != first:
                done = fence(done)
            row = GROUP * (d % 2 if d > 1 else 0)
            (done,) = cache_attention(
                asked[d], cols, asked[d], row, kvs, at, True, done
            )
            far.append(swap(done, d * GROUP))
            if i == len(offsets) - 3:
                weights = [output_weight] + [
                    turn(ordered(output_weight, done), step) for step in range(1, n_head)
                ]
        else:
            pair = cache_attention(
                queries, cols, fill_here, 0, kvs[:2], at[:2], False, done
            )
            near.append(pair)
            done = fence(pair[1], far[0])
            pass_on(d, done)
            kvs[3] = sibling[d]
            for part in (slice(2, 3), slice(3, 4)):
                pair = cache_attention(
                    queries, cols, fill_here, part.start, kvs[part], at[part], False, done
                )
                near.append(pair)
                done = pair[1]
        if i == 0:
            memory_read, new_state = memory_pass(
                side, shard_tokens, retention, momentum, memory_step_scale, halving_updates,
                done, queries, own_keys, own_values, memory_state[:, 0],
            )
            done = memory_read
    head_out = merge(near, far, projected, memory_read)

    layer = jnp.zeros((shard_tokens, width), f32)
    for step in range(n_head):
        away = (n_head - step) % n_head
        part = head_out[:, away * shard_tokens : (away + 1) * shard_tokens]
        if step:
            part = turn(part, step)
        layer = layer + dot(part, weights[step], ((0,), (0,))).astype(bf16).astype(f32)
    return (layer.astype(bf16)[None], new_state[:, None])


def solution(mesh):
    in_specs = (
        P("req", "head", None),
        P(),
        P(None, None, "head"),
        P("head", None),
        P(None, None, "head"),
        P("req", None, None, None, "head"),
        P("req"),
        P("req", None),
        P("req", None),
        P(None, "req", "head", None, None),
        P("req", "head"),
        P("req", "head"),
        P("req", "head"),
        P("req", None),
    )
    out_specs = (P("req", "head", None), P(None, "req", "head", None, None))
    return jax.shard_map(shards, mesh=mesh, in_specs=in_specs, out_specs=out_specs, check_vma=False)
```

```python
import functools
import math

import jax
import jax.numpy as jnp
from jax import lax
from jax.experimental import pallas as pl
from jax.experimental.pallas import tpu as pltpu
from jax.sharding import PartitionSpec as P

HD = 128
BLK = 64
PAGE = 32
GROUP = 4


norm_eps = 1e-05
unit_eps = 1e-06
LOG2E = math.log2(math.e)
MASKED = -1e30
LAST = pl.CostEstimate(flops=6 * 10**9, bytes_accessed=1, transcendentals=0)
VMEM_LIMIT = 16 * 2**20
TAIL = 16
f32 = jnp.float32
bf16 = jnp.bfloat16
COST = pl.CostEstimate(flops=1, bytes_accessed=1, transcendentals=0)


def dot(left, right, contract=((1,), (0,)), precision=None):
    return lax.dot_general(
        left, right, (contract, ((), ())), precision=precision, preferred_element_type=f32
    )


def fence_kernel(*refs):
    refs[-1][...] = jnp.zeros_like(refs[-1])


def fence(*earlier):
    return pl.pallas_call(
        fence_kernel,
        out_shape=jax.ShapeDtypeStruct((8, HD), f32),
        in_specs=[pl.BlockSpec(memory_space=pl.ANY)] * len(earlier),
        compiler_params=pltpu.CompilerParams(vmem_limit_bytes=2**20),
        cost_estimate=LAST,
    )(*earlier)


def deal_kernel(counts, at_ref, from_ref, after_ref, *refs):
    del after_ref
    outs, (held, into, out_of) = refs[: len(counts)], refs[len(counts) :]
    places = [(out, i) for count, out in zip(counts, outs) for i in range(count)]
    reads, writes = [], []
    for at, (out, i) in enumerate(places):
        reads.append(pltpu.make_async_copy(from_ref.at[at_ref[at]], held.at[at], into.at[at]))
        writes.append(pltpu.make_async_copy(held.at[at], out.at[i], out_of.at[at]))
    for copy in reads:
        copy.start()
    for read, write in zip(reads, writes):
        read.wait()
        write.start()
    for copy in writes:
        copy.wait()


def deal(source, hands, after, vmem_limit):
    counts = [len(rows) for rows in hands]
    total = sum(counts)
    anywhere = pl.BlockSpec(memory_space=pl.ANY)
    return pl.pallas_call(
        functools.partial(deal_kernel, counts),
        out_shape=[
            jax.ShapeDtypeStruct((count,) + source.shape[1:], source.dtype) for count in counts
        ],
        grid_spec=pltpu.PrefetchScalarGridSpec(
            num_scalar_prefetch=1,
            in_specs=[anywhere] * 2,
            out_specs=[anywhere] * len(counts),
            scratch_shapes=[
                pltpu.VMEM((total,) + source.shape[1:], source.dtype),
                pltpu.SemaphoreType.DMA((total,)),
                pltpu.SemaphoreType.DMA((total,)),
            ],
        ),
        compiler_params=pltpu.CompilerParams(vmem_limit_bytes=vmem_limit),
        cost_estimate=COST,
    )(jnp.stack([row for rows in hands for row in rows]), source, after)


def cache_kernel(shape, sent, at_ref, after_ref, q_ref, fill_ref, *refs):
    del after_ref
    span, heads, count, fill_row = shape
    kv_refs = refs[:count]
    outs = refs[count:-6]
    kept_ref, wide_ref, bias_ref, score_ref, tail_ref, sems = refs[-6:]
    scale = LOG2E / math.sqrt(HD)
    head = pl.program_id(0)

    @pl.when(head == 0)
    def _():
        copies = [
            pltpu.make_async_copy(kv_refs[g].at[at_ref[g]], kept_ref.at[g], sems.at[g])
            for g in range(count)
        ]
        for copy in copies:
            copy.start()
        row = lax.broadcasted_iota(jnp.int32, (span, HD), 0)
        lane = lax.broadcasted_iota(jnp.int32, (span, HD), 1)
        slot = jnp.where(row // PAGE == lane, 1.0, 0.0).astype(bf16)
        filled = dot(slot, fill_ref[...], ((1,), (1,)))
        row_f = (row % PAGE).astype(f32)
        tail_ref[...] = jnp.zeros_like(tail_ref)
        for g in range(count):
            column = filled[:, fill_row + g : fill_row + g + 1]
            bias_ref[pl.ds(g * span, span), :] = jnp.where(row_f < column, 0.0, MASKED)
            copies[g].wait()
            wide_ref[g] = kept_ref[g].astype(f32)

    def part_of(g, which):
        rows = pl.ds(2 * head + which, span, stride=2 * heads)
        return wide_ref[g, rows, :].astype(bf16)

    q = q_ref[...]
    tokens = q.shape[1]
    top = jnp.full((1, tokens), MASKED, f32)
    for g in range(count):
        rows = pl.ds(g * span, span)
        score = dot(part_of(g, 0), q) * scale + jnp.tile(bias_ref[rows, :], (1, tokens // HD))
        score_ref[rows, :] = score
        top = jnp.maximum(top, jnp.max(score, axis=0, keepdims=True))
    total = jnp.zeros((1, tokens), f32)
    mixed = jnp.zeros((HD, tokens), f32)
    for g in range(count):
        rows = pl.ds(g * span, span)
        weight = jnp.exp2(score_ref[rows, :] - top)
        total = total + jnp.sum(weight, axis=0, keepdims=True)
        mixed = mixed + dot(part_of(g, 1), weight.astype(bf16), ((0,), (0,)))
    attended = mixed / total
    lse = top + jnp.log2(total)
    if sent:
        (out,) = outs
        rows = pl.ds(pl.multiple_of(head * HD, HD), HD)
        out[rows, :] = attended.astype(bf16)
        high = lse.astype(bf16).astype(f32)
        middle = (lse - high).astype(bf16).astype(f32)
        for i, term in enumerate((high, middle, lse - high - middle)):
            tail_ref[pl.ds(i * heads + head, 1), :] = term

        @pl.when(head == heads - 1)
        def _():
            out[pl.ds(heads * HD, TAIL), :] = tail_ref[...].astype(bf16)
    else:
        outs[0][0] = attended
        outs[1][0] = lse


def cache_attention(queries, cols, fill, fill_row, kvs, at, sent, after):
    count = len(kvs)
    heads = cols // HD
    span = kvs[0].shape[1] // (2 * heads)
    tokens = queries.shape[1]
    fill_at = cols // TAIL if fill.shape[0] > TAIL else 0

    def head_spec(*block):
        return pl.BlockSpec((1,) + block, lambda h, at: (h, 0, 0))

    if sent:
        out_shape = (jax.ShapeDtypeStruct((cols + TAIL, tokens), bf16),)
        out_specs = (pl.BlockSpec((cols + TAIL, tokens), lambda h, at: (0, 0)),)
    else:
        out_shape = (
            jax.ShapeDtypeStruct((heads, HD, tokens), f32),
            jax.ShapeDtypeStruct((heads, 1, tokens), f32),
        )
        out_specs = (head_spec(HD, tokens), head_spec(1, tokens))
    return pl.pallas_call(
        functools.partial(cache_kernel, (span, heads, count, fill_row), sent),
        out_shape=out_shape,
        grid_spec=pltpu.PrefetchScalarGridSpec(
            num_scalar_prefetch=1,
            grid=(heads,),
            in_specs=[
                pl.BlockSpec(memory_space=pl.ANY),
                pl.BlockSpec((HD, tokens), lambda h, at: (h, 0)),
                pl.BlockSpec((TAIL, HD), lambda h, at: (fill_at, 0)),
            ]
            + [pl.BlockSpec(memory_space=pl.ANY)] * count,
            out_specs=out_specs,
            scratch_shapes=[
                pltpu.VMEM((count,) + kvs[0].shape[1:], bf16),
                pltpu.VMEM((count,) + kvs[0].shape[1:], f32),
                pltpu.VMEM((count * span, HD), f32),
                pltpu.VMEM((count * span, tokens), f32),
                pltpu.VMEM((TAIL, tokens), f32),
                pltpu.SemaphoreType.DMA((count,)),
            ],
        ),
        compiler_params=pltpu.CompilerParams(vmem_limit_bytes=VMEM_LIMIT),
        cost_estimate=COST,
    )(jnp.stack(at), after, queries, fill, *kvs)


def own_kernel(shard, shards_in_all, side_ref, q_ref, k_ref, v_ref, persist_ref, att_ref, lse_ref):
    def place(axis):
        at = lax.broadcasted_iota(jnp.int32, (tokens, tokens), axis)
        return lax.rem(side_ref[0] + at // shard, shards_in_all) * shard + lax.rem(at, shard)

    scale = LOG2E / math.sqrt(HD)
    q = q_ref[...]
    tokens = q.shape[1]
    score_p = dot(persist_ref[0], q) * scale
    score_t = dot(k_ref[...].T, q) * scale
    score_t = jnp.where(place(0) <= place(1), score_t, MASKED)
    top = jnp.maximum(
        jnp.max(score_p, axis=0, keepdims=True), jnp.max(score_t, axis=0, keepdims=True)
    )
    weight_p = jnp.exp2(score_p - top)
    weight_t = jnp.exp2(score_t - top)
    total = jnp.sum(weight_p, axis=0, keepdims=True) + jnp.sum(weight_t, axis=0, keepdims=True)
    mixed = dot(v_ref[...], weight_t.astype(bf16)) + dot(
        persist_ref[1], weight_p.astype(bf16), ((0,), (0,))
    )
    att_ref[0] = mixed / total
    lse_ref[0] = top + jnp.log2(total)


def own_attention(side, shard, q, k, v, persist):
    cols, tokens = q.shape
    heads = cols // HD
    head_spec = pl.BlockSpec((HD, tokens), lambda h: (h, 0))
    return pl.pallas_call(
        functools.partial(own_kernel, shard, tokens // shard),
        out_shape=(
            jax.ShapeDtypeStruct((heads, HD, tokens), f32),
            jax.ShapeDtypeStruct((heads, 1, tokens), f32),
        ),
        grid=(heads,),
        in_specs=[pl.BlockSpec(memory_space=pltpu.SMEM)]
        + [head_spec] * 3
        + [pl.BlockSpec((2, persist.shape[1], HD), lambda h: (0, 0, h))],
        out_specs=(
            pl.BlockSpec((1, HD, tokens), lambda h: (h, 0, 0)),
            pl.BlockSpec((1, 1, tokens), lambda h: (h, 0, 0)),
        ),
        compiler_params=pltpu.CompilerParams(vmem_limit_bytes=VMEM_LIMIT),
        cost_estimate=COST,
    )(side[None], q, k, v, persist)


def memory_kernel(
    shards_in_all, side_ref, retention_ref, momentum_ref, step_ref, halving_ref, after_ref,
    q_ref, k_ref, v_ref, state_ref, read_ref, new_ref, kn_ref,
):
    del after_ref
    heads = state_ref.shape[1]
    tokens = q_ref.shape[1]
    shard = tokens // shards_in_all
    exact = lax.Precision.HIGHEST
    ms = [state_ref[0, h] for h in range(heads)]
    ss = [state_ref[1, h] for h in range(heads)]
    for a in range(shards_in_all):
        start = lax.rem(a + shards_in_all - side_ref[0], shards_in_all) * shard
        lanes = slice(None) if shards_in_all == 1 else pl.ds(pl.multiple_of(start, HD), shard)
        units = []
        for h in range(heads):
            rows = pl.ds(h * HD, HD)
            q = q_ref[rows, lanes].astype(f32)
            k = k_ref[rows, lanes].astype(f32)
            qn = q * lax.rsqrt(jnp.sum(q * q, axis=0, keepdims=True) + unit_eps)
            kn = k * lax.rsqrt(jnp.sum(k * k, axis=0, keepdims=True) + unit_eps)
            kn_ref[h] = kn.T
            units.append((qn, kn, v_ref[rows, lanes].astype(f32), []))
        for b in range(shard // BLK):
            lower, upper = b * BLK, (b + 1) * BLK
            for h in range(heads):
                qn, kn, values, reads = units[h]
                both = jnp.concatenate([kn[:, lower:upper], qn[:, lower:upper]], axis=1)
                product = dot(ms[h], both, precision=exact)
                error = product[:, :BLK] - values[:, lower:upper]
                reads.append(product[:, BLK:])
                grad = dot(error, kn_ref[h, lower:upper, :], precision=exact)
                ss[h] = momentum_ref[0, h] * ss[h] - step_ref[0, h] * grad
                halving = halving_ref[0, a * (shard // BLK) + b]
                keep = retention_ref[0, h] * jnp.where(halving == 1, 0.5, 1.0)
                ms[h] = keep * ms[h] + ss[h]
        for h in range(heads):
            read_ref[pl.ds(h * HD, HD), lanes] = jnp.concatenate(units[h][3], axis=1)
    for h in range(heads):
        new_ref[0, h] = ms[h]
        new_ref[1, h] = ss[h]


def memory_pass(side, shard, retention, momentum, step, halving, after, q, k, v, state):
    cols, tokens = q.shape
    heads = cols // HD
    count = tokens // shard if shard % HD == 0 else 1

    def rolled(value, shift):
        twice = jnp.concatenate([value, value], axis=1)
        return lax.dynamic_slice_in_dim(twice, shift * shard, tokens, 1)

    if count == 1:
        back = (tokens // shard - side) % (tokens // shard)
        q, k, v = rolled(q, back), rolled(k, back), rolled(v, back)
    smem = pl.BlockSpec(memory_space=pltpu.SMEM)
    vmem = pl.BlockSpec(memory_space=pltpu.VMEM)
    read, new = pl.pallas_call(
        functools.partial(memory_kernel, count),
        out_shape=(
            jax.ShapeDtypeStruct((cols, tokens), f32),
            jax.ShapeDtypeStruct(state.shape, f32),
        ),
        in_specs=[smem] * 5 + [pl.BlockSpec(memory_space=pl.ANY)] + [vmem] * 4,
        out_specs=(vmem, vmem),
        scratch_shapes=[pltpu.VMEM((heads, tokens // count, HD), f32)],
        compiler_params=pltpu.CompilerParams(vmem_limit_bytes=VMEM_LIMIT),
        cost_estimate=COST,
    )(side[None], retention, momentum, step, halving, after, q, k, v, state)
    return (read if count > 1 else rolled(read, side)), new


def merge_kernel(near, heads, *refs):
    pairs = [(refs[2 * i][0], refs[2 * i + 1][0]) for i in range(near)]
    for att, tail in zip(refs[2 * near : -3 : 2], refs[2 * near + 1 : -3 : 2]):
        row = lax.broadcasted_iota(jnp.int32, tail.shape, 0)
        mine = (lax.rem(row, heads) == pl.program_id(0)) & (row < 3 * heads)
        lse = jnp.sum(jnp.where(mine, tail[...].astype(f32), 0.0), axis=0, keepdims=True)
        pairs.append((att[...].astype(f32), lse))
    gate_ref, read_ref, out_ref = refs[-3:]
    top = functools.reduce(jnp.maximum, [lse for _, lse in pairs])
    total = jnp.zeros_like(top)
    mixed = jnp.zeros(out_ref.shape, f32)
    for att, lse in pairs:
        share = jnp.exp2(lse - top)
        total = total + share
        mixed = mixed + att * share
    attended = mixed / total
    unit = attended * lax.rsqrt(jnp.mean(attended * attended, axis=0, keepdims=True) + unit_eps)
    gate = 1.0 / (1.0 + jnp.exp(-gate_ref[...]))
    out_ref[...] = (unit + gate * read_ref[...]).astype(bf16)


def merge(near, far, projected, read):
    cols, tokens = read.shape
    heads = cols // HD
    gates = projected.shape[0] // HD - heads
    flat_spec = pl.BlockSpec((HD, tokens), lambda h: (h, 0))

    def head_spec(*block):
        return pl.BlockSpec((1,) + block, lambda h: (h, 0, 0))

    return pl.pallas_call(
        functools.partial(merge_kernel, len(near), heads),
        out_shape=jax.ShapeDtypeStruct((cols, tokens), bf16),
        grid=(heads,),
        in_specs=[head_spec(HD, tokens), head_spec(1, tokens)] * len(near)
        + [flat_spec, pl.BlockSpec((TAIL, tokens), lambda h: (cols // TAIL, 0))] * len(far)
        + [pl.BlockSpec((HD, tokens), lambda h: (gates + h, 0)), flat_spec],
        out_specs=flat_spec,
        compiler_params=pltpu.CompilerParams(vmem_limit_bytes=VMEM_LIMIT),
        cost_estimate=pl.CostEstimate(
            flops=10 * (len(near) + len(far)) * cols * tokens,
            bytes_accessed=(4 * len(near) + 2 * len(far) + 10) * cols * tokens,
            transcendentals=cols * tokens,
        ),
    )(*(value for pair in near for value in pair), *(f for f in far for _ in (0, 1)), projected, read)


def shards(
    tokens,
    gain,
    projection_weight,
    output_weight,
    persist,
    cache_page_slots,
    cached_length,
    page_keeper,
    page_slot_index,
    memory_state,
    retention,
    momentum,
    memory_step_scale,
    halving_updates,
):
    shard_tokens = tokens.shape[1]
    width = tokens.shape[2]
    cols = projection_weight.shape[2]
    devices = cache_page_slots.shape[1]
    span = cache_page_slots.shape[2]
    lanes = span // PAGE
    max_pages = page_keeper.shape[1]
    planes = devices // GROUP
    n_head = lax.axis_size("head")
    here = lax.axis_index("req")
    plane, place = here // GROUP, here % GROUP
    side = lax.axis_index("head")

    def swap(value, step):
        return lax.ppermute(value, "req", [(i, i ^ step) for i in range(devices)])

    def turn(value, step):
        return lax.ppermute(
            value, "head", [(i, (i - step) % n_head) for i in range(n_head)]
        )

    def projection(rows, weight):
        return dot(weight, rows, ((0,), (1,)))

    def norm(rows):
        x = rows.astype(f32)
        return (
            x * lax.rsqrt(jnp.mean(x * x, axis=-1, keepdims=True) + norm_eps) * gain.astype(f32)
        ).astype(bf16)

    def ordered(value, *earlier):
        return lax.optimization_barrier((value,) + earlier)[0]

    others = [turn(tokens[0], step) for step in range(1, n_head)]

    page_ids = jnp.arange(max_pages, dtype=jnp.int32)
    filled = jnp.clip(cached_length[0] - page_ids * PAGE, 0, PAGE)
    slot_of = page_keeper[0] * lanes + page_slot_index[0]
    keeper = (plane ^ jnp.arange(planes, dtype=jnp.int32))[:, None] * GROUP + (
        place ^ jnp.arange(GROUP, dtype=jnp.int32)
    )
    slot_ids = keeper[:, :, None] * lanes + jnp.arange(lanes, dtype=jnp.int32)
    slot_fill = jnp.sum(
        jnp.where(slot_of == slot_ids[..., None], filled, 0), axis=-1
    )

    offsets = list(range(2, planes)) + [1, 0]
    core = place % 2
    cache = cache_page_slots[0]
    heads = cols // HD
    cache = cache.reshape(devices, span, 2, heads, HD).transpose(0, 1, 3, 2, 4)
    cache = cache.reshape(devices, span * heads * 2, HD)

    hands = []
    for d in offsets:
        start = (plane ^ d) * GROUP + ((place // 2) ^ 1) * 2
        hands.append([start, start + 1])
    for k in (1, 0):
        hands.append([z * GROUP + (place ^ k) for z in range(planes)])
    pieces = dict(zip(offsets, deal(cache, hands[:1], gain, 56 * 2**20)))

    def with_fill(value, d):
        rows = jnp.concatenate([slot_fill[d], slot_fill[d ^ 1]], axis=0)
        tail = TAIL if d == 1 else 2 * TAIL
        rows = jnp.pad(rows, ((0, tail - 2 * GROUP), (0, value.shape[1] - lanes)))
        return jnp.concatenate([value, rows.astype(bf16)], axis=0)

    across, sibling, far_here, far_rest = {}, {}, {}, {}

    def pass_on(d, *earlier):
        piece = ordered(across[d], *earlier)
        if d:
            (piece,) = deal(piece, [[1 - core]], gain, 2 * 2**20)
        else:
            piece = lax.dynamic_index_in_dim(piece, 1 - core, 0)
        sibling[d] = swap(piece, 1)

    first, second = offsets[:2]
    across[first] = swap(pieces[first], 2)
    flat = ordered(projection_weight, pieces[first]).reshape(width, 4 * cols)
    normed_here = norm(tokens[0])
    query_here = projection(normed_here, flat[:, :cols]).astype(bf16)
    far_here[first] = swap(with_fill(query_here, first), first * GROUP)
    far_here[1] = swap(with_fill(query_here, 1), GROUP)
    normed_rest = norm(ordered(jnp.concatenate(others, axis=0), query_here))
    query_rest = projection(normed_rest, flat[:, :cols]).astype(bf16)
    far_rest[first] = swap(query_rest, first * GROUP)
    *rest, column, own = deal(cache, hands[1:], query_rest, 56 * 2**20)
    pieces |= zip(offsets[1:], rest)
    across[second] = swap(pieces[second], 2)
    beside = swap(column, 1)
    projected = projection(
        jnp.concatenate([normed_here, normed_rest], axis=0), ordered(flat, query_rest)[:, cols:]
    )
    queries = jnp.concatenate([query_here, query_rest], axis=1)
    own_keys = projected[:cols].astype(bf16)
    own_values = projected[cols : 2 * cols].astype(bf16)
    far_rest[1] = swap(ordered(query_rest, far_here[1], own_values), GROUP)

    att, lse = own_attention(side, shard_tokens, queries, own_keys, own_values, persist)
    near, far = [(att, lse)], []
    fill_here = jnp.pad(slot_fill[0], ((0, TAIL - GROUP), (0, HD - lanes))).astype(bf16)
    pass_on(first, lse)

    def whole_of(d):
        rest_rows = ((0, far_here[d].shape[0] - cols), (0, 0))
        rest_rows = jnp.pad(far_rest[d], rest_rows)
        return jnp.concatenate([far_here[d], rest_rows], axis=1)

    asked = {}
    done = fence(lse)
    for i, d in enumerate(offsets):
        if i and d:
            pass_on(d, done)
        if d == 1:
            asked[1] = whole_of(1)
        if d and d % 2 == 0:
            if d not in far_here:
                far_here[d] = swap(with_fill(ordered(query_here, done), d), d * GROUP)
                far_rest[d] = swap(ordered(query_rest, done), d * GROUP)
            asked[d] = whole_of(d)
            asked[d ^ 1] = swap(asked[d], GROUP)
        if i + 2 < len(offsets):
            earlier = [across[d], far_here[d], far_rest[d]] if i == 0 else [done, far_rest[1]]
            across[offsets[i + 2]] = swap(ordered(pieces[offsets[i + 2]], *earlier), 2)
        kvs = [own, beside, across[d], sibling.get(d)]
        at = [plane ^ d, plane ^ d, core, jnp.zeros_like(core)]
        if d:
            if d != first:
                done = fence(done)
            row = GROUP * (d % 2 if d > 1 else 0)
            (done,) = cache_attention(
                asked[d], cols, asked[d], row, kvs, at, True, done
            )
            far.append(swap(done, d * GROUP))
            if i == len(offsets) - 3:
                weights = [output_weight] + [
                    turn(ordered(output_weight, done), step) for step in range(1, n_head)
                ]
        else:
            pair = cache_attention(
                queries, cols, fill_here, 0, kvs[:2], at[:2], False, done
            )
            near.append(pair)
            done = fence(pair[1], far[0])
            pass_on(d, done)
            kvs[3] = sibling[d]
            for part in (slice(2, 3), slice(3, 4)):
                pair = cache_attention(
                    queries, cols, fill_here, part.start, kvs[part], at[part], False, done
                )
                near.append(pair)
                done = pair[1]
        if i == 0:
            memory_read, new_state = memory_pass(
                side, shard_tokens, retention, momentum, memory_step_scale, halving_updates,
                done, queries, own_keys, own_values, memory_state[:, 0],
            )
            done = memory_read
    head_out = merge(near, far, projected, memory_read)

    layer = jnp.zeros((shard_tokens, width), f32)
    for step in range(n_head):
        away = (n_head - step) % n_head
        part = head_out[:, away * shard_tokens : (away + 1) * shard_tokens]
        if step:
            part = turn(part, step)
        layer = layer + dot(part, weights[step], ((0,), (0,))).astype(bf16).astype(f32)
    return (layer.astype(bf16)[None], new_state[:, None])


def solution(mesh):
    in_specs = (
        P("req", "head", None),
        P(),
        P(None, None, "head"),
        P("head", None),
        P(None, None, "head"),
        P("req", None, None, None, "head"),
        P("req"),
        P("req", None),
        P("req", None),
        P(None, "req", "head", None, None),
        P("req", "head"),
        P("req", "head"),
        P("req", "head"),
        P("req", None),
    )
    out_specs = (P("req", "head", None), P(None, "req", "head", None, None))
    return jax.shard_map(shards, mesh=mesh, in_specs=in_specs, out_specs=out_specs, check_vma=False)
```

```python
import functools
import math

import jax
import jax.numpy as jnp
from jax import lax
from jax.experimental import pallas as pl
from jax.experimental.pallas import tpu as pltpu
from jax.sharding import PartitionSpec as P

HD = 128
BLK = 64
PAGE = 32
GROUP = 4


norm_eps = 1e-05
unit_eps = 1e-06
LOG2E = math.log2(math.e)
MASKED = -1e30
LAST = pl.CostEstimate(flops=6 * 10**9, bytes_accessed=1, transcendentals=0)
VMEM_LIMIT = 16 * 2**20
TAIL = 16
f32 = jnp.float32
bf16 = jnp.bfloat16
COST = pl.CostEstimate(flops=1, bytes_accessed=1, transcendentals=0)


def dot(left, right, contract=((1,), (0,)), precision=None):
    return lax.dot_general(
        left, right, (contract, ((), ())), precision=precision, preferred_element_type=f32
    )


def fence_kernel(*refs):
    refs[-1][...] = jnp.zeros_like(refs[-1])


def fence(*earlier):
    return pl.pallas_call(
        fence_kernel,
        out_shape=jax.ShapeDtypeStruct((8, HD), f32),
        in_specs=[pl.BlockSpec(memory_space=pl.ANY)] * len(earlier),
        compiler_params=pltpu.CompilerParams(vmem_limit_bytes=2**20),
        cost_estimate=LAST,
    )(*earlier)


def deal_kernel(counts, at_ref, from_ref, after_ref, *refs):
    del after_ref
    outs, (held, into, out_of) = refs[: len(counts)], refs[len(counts) :]
    places = [(out, i) for count, out in zip(counts, outs) for i in range(count)]
    reads, writes = [], []
    for at, (out, i) in enumerate(places):
        reads.append(pltpu.make_async_copy(from_ref.at[at_ref[at]], held.at[at], into.at[at]))
        writes.append(pltpu.make_async_copy(held.at[at], out.at[i], out_of.at[at]))
    for copy in reads:
        copy.start()
    for read, write in zip(reads, writes):
        read.wait()
        write.start()
    for copy in writes:
        copy.wait()


def deal(source, hands, after, vmem_limit):
    counts = [len(rows) for rows in hands]
    total = sum(counts)
    anywhere = pl.BlockSpec(memory_space=pl.ANY)
    return pl.pallas_call(
        functools.partial(deal_kernel, counts),
        out_shape=[
            jax.ShapeDtypeStruct((count,) + source.shape[1:], source.dtype) for count in counts
        ],
        grid_spec=pltpu.PrefetchScalarGridSpec(
            num_scalar_prefetch=1,
            in_specs=[anywhere] * 2,
            out_specs=[anywhere] * len(counts),
            scratch_shapes=[
                pltpu.VMEM((total,) + source.shape[1:], source.dtype),
                pltpu.SemaphoreType.DMA((total,)),
                pltpu.SemaphoreType.DMA((total,)),
            ],
        ),
        compiler_params=pltpu.CompilerParams(vmem_limit_bytes=vmem_limit),
        cost_estimate=COST,
    )(jnp.stack([row for rows in hands for row in rows]), source, after)


def cache_kernel(shape, sent, at_ref, after_ref, q_ref, fill_ref, *refs):
    del after_ref
    span, heads, count, fill_row = shape
    kv_refs = refs[:count]
    outs = refs[count:-6]
    kept_ref, wide_ref, bias_ref, score_ref, tail_ref, sems = refs[-6:]
    scale = LOG2E / math.sqrt(HD)
    head = pl.program_id(0)

    @pl.when(head == 0)
    def _():
        copies = [
            pltpu.make_async_copy(kv_refs[g].at[at_ref[g]], kept_ref.at[g], sems.at[g])
            for g in range(count)
        ]
        for copy in copies:
            copy.start()
        row = lax.broadcasted_iota(jnp.int32, (span, HD), 0)
        lane = lax.broadcasted_iota(jnp.int32, (span, HD), 1)
        slot = jnp.where(row // PAGE == lane, 1.0, 0.0).astype(bf16)
        filled = dot(slot, fill_ref[...], ((1,), (1,)))
        row_f = (row % PAGE).astype(f32)
        tail_ref[...] = jnp.zeros_like(tail_ref)
        for g in range(count):
            column = filled[:, fill_row + g : fill_row + g + 1]
            bias_ref[pl.ds(g * span, span), :] = jnp.where(row_f < column, 0.0, MASKED)
            copies[g].wait()
            wide_ref[g, pl.ds(0, 2 * heads * span), :] = kept_ref[g].astype(f32)

    def part_of(g, which):
        rows = pl.ds(2 * head + which, span, stride=2 * heads)
        return wide_ref[g, rows, :].astype(bf16)

    q = q_ref[...]
    tokens = q.shape[1]
    top = jnp.full((1, tokens), MASKED, f32)
    for g in range(count):
        rows = pl.ds(g * span, span)
        score = dot(part_of(g, 0), q) * scale + jnp.tile(bias_ref[rows, :], (1, tokens // HD))
        score_ref[rows, :] = score
        top = jnp.maximum(top, jnp.max(score, axis=0, keepdims=True))
    total = jnp.zeros((1, tokens), f32)
    mixed = jnp.zeros((HD, tokens), f32)
    for g in range(count):
        rows = pl.ds(g * span, span)
        weight = jnp.exp2(score_ref[rows, :] - top)
        total = total + jnp.sum(weight, axis=0, keepdims=True)
        mixed = mixed + dot(part_of(g, 1), weight.astype(bf16), ((0,), (0,)))
    attended = mixed / total
    lse = top + jnp.log2(total)
    if sent:
        (out,) = outs
        rows = pl.ds(pl.multiple_of(head * HD, HD), HD)
        out[rows, :] = attended.astype(bf16)
        high = lse.astype(bf16).astype(f32)
        middle = (lse - high).astype(bf16).astype(f32)
        for i, term in enumerate((high, middle, lse - high - middle)):
            tail_ref[pl.ds(i * heads + head, 1), :] = term

        @pl.when(head == heads - 1)
        def _():
            out[pl.ds(heads * HD, TAIL), :] = tail_ref[...].astype(bf16)
    else:
        outs[0][0] = attended
        outs[1][0] = lse


def cache_attention(queries, cols, fill, fill_row, kvs, at, sent, after):
    count = len(kvs)
    heads = cols // HD
    span = kvs[0].shape[1] // (2 * heads)
    tokens = queries.shape[1]
    fill_at = cols // TAIL if fill.shape[0] > TAIL else 0

    def head_spec(*block):
        return pl.BlockSpec((1,) + block, lambda h, at: (h, 0, 0))

    if sent:
        out_shape = (jax.ShapeDtypeStruct((cols + TAIL, tokens), bf16),)
        out_specs = (pl.BlockSpec((cols + TAIL, tokens), lambda h, at: (0, 0)),)
    else:
        out_shape = (
            jax.ShapeDtypeStruct((heads, HD, tokens), f32),
            jax.ShapeDtypeStruct((heads, 1, tokens), f32),
        )
        out_specs = (head_spec(HD, tokens), head_spec(1, tokens))
    return pl.pallas_call(
        functools.partial(cache_kernel, (span, heads, count, fill_row), sent),
        out_shape=out_shape,
        grid_spec=pltpu.PrefetchScalarGridSpec(
            num_scalar_prefetch=1,
            grid=(heads,),
            in_specs=[
                pl.BlockSpec(memory_space=pl.ANY),
                pl.BlockSpec((HD, tokens), lambda h, at: (h, 0)),
                pl.BlockSpec((TAIL, HD), lambda h, at: (fill_at, 0)),
            ]
            + [pl.BlockSpec(memory_space=pl.ANY)] * count,
            out_specs=out_specs,
            scratch_shapes=[
                pltpu.VMEM((count,) + kvs[0].shape[1:], bf16),
                pltpu.VMEM((count, 2 * heads * (span + 1), HD), f32),
                pltpu.VMEM((count * span, HD), f32),
                pltpu.VMEM((count * span, tokens), f32),
                pltpu.VMEM((TAIL, tokens), f32),
                pltpu.SemaphoreType.DMA((count,)),
            ],
        ),
        compiler_params=pltpu.CompilerParams(vmem_limit_bytes=VMEM_LIMIT),
        cost_estimate=COST,
    )(jnp.stack(at), after, queries, fill, *kvs)


def own_kernel(shard, shards_in_all, side_ref, q_ref, k_ref, v_ref, persist_ref, att_ref, lse_ref):
    def place(axis):
        at = lax.broadcasted_iota(jnp.int32, (tokens, tokens), axis)
        return lax.rem(side_ref[0] + at // shard, shards_in_all) * shard + lax.rem(at, shard)

    scale = LOG2E / math.sqrt(HD)
    q = q_ref[...]
    tokens = q.shape[1]
    score_p = dot(persist_ref[0], q) * scale
    score_t = dot(k_ref[...].T, q) * scale
    score_t = jnp.where(place(0) <= place(1), score_t, MASKED)
    top = jnp.maximum(
        jnp.max(score_p, axis=0, keepdims=True), jnp.max(score_t, axis=0, keepdims=True)
    )
    weight_p = jnp.exp2(score_p - top)
    weight_t = jnp.exp2(score_t - top)
    total = jnp.sum(weight_p, axis=0, keepdims=True) + jnp.sum(weight_t, axis=0, keepdims=True)
    mixed = dot(v_ref[...], weight_t.astype(bf16)) + dot(
        persist_ref[1], weight_p.astype(bf16), ((0,), (0,))
    )
    att_ref[0] = mixed / total
    lse_ref[0] = top + jnp.log2(total)


def own_attention(side, shard, q, k, v, persist):
    cols, tokens = q.shape
    heads = cols // HD
    head_spec = pl.BlockSpec((HD, tokens), lambda h: (h, 0))
    return pl.pallas_call(
        functools.partial(own_kernel, shard, tokens // shard),
        out_shape=(
            jax.ShapeDtypeStruct((heads, HD, tokens), f32),
            jax.ShapeDtypeStruct((heads, 1, tokens), f32),
        ),
        grid=(heads,),
        in_specs=[pl.BlockSpec(memory_space=pltpu.SMEM)]
        + [head_spec] * 3
        + [pl.BlockSpec((2, persist.shape[1], HD), lambda h: (0, 0, h))],
        out_specs=(
            pl.BlockSpec((1, HD, tokens), lambda h: (h, 0, 0)),
            pl.BlockSpec((1, 1, tokens), lambda h: (h, 0, 0)),
        ),
        compiler_params=pltpu.CompilerParams(vmem_limit_bytes=VMEM_LIMIT),
        cost_estimate=COST,
    )(side[None], q, k, v, persist)


def memory_kernel(
    shards_in_all, side_ref, retention_ref, momentum_ref, step_ref, halving_ref, after_ref,
    q_ref, k_ref, v_ref, state_ref, read_ref, new_ref, kn_ref,
):
    del after_ref
    heads = state_ref.shape[1]
    tokens = q_ref.shape[1]
    shard = tokens // shards_in_all
    exact = lax.Precision.HIGHEST
    ms = [state_ref[0, h] for h in range(heads)]
    ss = [state_ref[1, h] for h in range(heads)]
    for a in range(shards_in_all):
        start = lax.rem(a + shards_in_all - side_ref[0], shards_in_all) * shard
        lanes = slice(None) if shards_in_all == 1 else pl.ds(pl.multiple_of(start, HD), shard)
        units = []
        for h in range(heads):
            rows = pl.ds(h * HD, HD)
            q = q_ref[rows, lanes].astype(f32)
            k = k_ref[rows, lanes].astype(f32)
            qn = q * lax.rsqrt(jnp.sum(q * q, axis=0, keepdims=True) + unit_eps)
            kn = k * lax.rsqrt(jnp.sum(k * k, axis=0, keepdims=True) + unit_eps)
            kn_ref[h] = kn.T
            units.append((qn, kn, v_ref[rows, lanes].astype(f32), []))
        for b in range(shard // BLK):
            lower, upper = b * BLK, (b + 1) * BLK
            for h in range(heads):
                qn, kn, values, reads = units[h]
                both = jnp.concatenate([kn[:, lower:upper], qn[:, lower:upper]], axis=1)
                product = dot(ms[h], both, precision=exact)
                error = product[:, :BLK] - values[:, lower:upper]
                reads.append(product[:, BLK:])
                grad = dot(error, kn_ref[h, lower:upper, :], precision=exact)
                ss[h] = momentum_ref[0, h] * ss[h] - step_ref[0, h] * grad
                halving = halving_ref[0, a * (shard // BLK) + b]
                keep = retention_ref[0, h] * jnp.where(halving == 1, 0.5, 1.0)
                ms[h] = keep * ms[h] + ss[h]
        for h in range(heads):
            read_ref[pl.ds(h * HD, HD), lanes] = jnp.concatenate(units[h][3], axis=1)
    for h in range(heads):
        new_ref[0, h] = ms[h]
        new_ref[1, h] = ss[h]


def memory_pass(side, shard, retention, momentum, step, halving, after, q, k, v, state):
    cols, tokens = q.shape
    heads = cols // HD
    count = tokens // shard if shard % HD == 0 else 1

    def rolled(value, shift):
        twice = jnp.concatenate([value, value], axis=1)
        return lax.dynamic_slice_in_dim(twice, shift * shard, tokens, 1)

    if count == 1:
        back = (tokens // shard - side) % (tokens // shard)
        q, k, v = rolled(q, back), rolled(k, back), rolled(v, back)
    smem = pl.BlockSpec(memory_space=pltpu.SMEM)
    vmem = pl.BlockSpec(memory_space=pltpu.VMEM)
    read, new = pl.pallas_call(
        functools.partial(memory_kernel, count),
        out_shape=(
            jax.ShapeDtypeStruct((cols, tokens), f32),
            jax.ShapeDtypeStruct(state.shape, f32),
        ),
        in_specs=[smem] * 5 + [pl.BlockSpec(memory_space=pl.ANY)] + [vmem] * 4,
        out_specs=(vmem, vmem),
        scratch_shapes=[pltpu.VMEM((heads, tokens // count, HD), f32)],
        compiler_params=pltpu.CompilerParams(vmem_limit_bytes=VMEM_LIMIT),
        cost_estimate=COST,
    )(side[None], retention, momentum, step, halving, after, q, k, v, state)
    return (read if count > 1 else rolled(read, side)), new


def merge_kernel(near, heads, *refs):
    pairs = [(refs[2 * i][0], refs[2 * i + 1][0]) for i in range(near)]
    for att, tail in zip(refs[2 * near : -3 : 2], refs[2 * near + 1 : -3 : 2]):
        row = lax.broadcasted_iota(jnp.int32, tail.shape, 0)
        mine = (lax.rem(row, heads) == pl.program_id(0)) & (row < 3 * heads)
        lse = jnp.sum(jnp.where(mine, tail[...].astype(f32), 0.0), axis=0, keepdims=True)
        pairs.append((att[...].astype(f32), lse))
    gate_ref, read_ref, out_ref = refs[-3:]
    top = functools.reduce(jnp.maximum, [lse for _, lse in pairs])
    total = jnp.zeros_like(top)
    mixed = jnp.zeros(out_ref.shape, f32)
    for att, lse in pairs:
        share = jnp.exp2(lse - top)
        total = total + share
        mixed = mixed + att * share
    attended = mixed / total
    unit = attended * lax.rsqrt(jnp.mean(attended * attended, axis=0, keepdims=True) + unit_eps)
    gate = 1.0 / (1.0 + jnp.exp(-gate_ref[...]))
    out_ref[...] = (unit + gate * read_ref[...]).astype(bf16)


def merge(near, far, projected, read):
    cols, tokens = read.shape
    heads = cols // HD
    gates = projected.shape[0] // HD - heads
    flat_spec = pl.BlockSpec((HD, tokens), lambda h: (h, 0))

    def head_spec(*block):
        return pl.BlockSpec((1,) + block, lambda h: (h, 0, 0))

    return pl.pallas_call(
        functools.partial(merge_kernel, len(near), heads),
        out_shape=jax.ShapeDtypeStruct((cols, tokens), bf16),
        grid=(heads,),
        in_specs=[head_spec(HD, tokens), head_spec(1, tokens)] * len(near)
        + [flat_spec, pl.BlockSpec((TAIL, tokens), lambda h: (cols // TAIL, 0))] * len(far)
        + [pl.BlockSpec((HD, tokens), lambda h: (gates + h, 0)), flat_spec],
        out_specs=flat_spec,
        compiler_params=pltpu.CompilerParams(vmem_limit_bytes=VMEM_LIMIT),
        cost_estimate=pl.CostEstimate(
            flops=10 * (len(near) + len(far)) * cols * tokens,
            bytes_accessed=(4 * len(near) + 2 * len(far) + 10) * cols * tokens,
            transcendentals=cols * tokens,
        ),
    )(*(value for pair in near for value in pair), *(f for f in far for _ in (0, 1)), projected, read)


def shards(
    tokens,
    gain,
    projection_weight,
    output_weight,
    persist,
    cache_page_slots,
    cached_length,
    page_keeper,
    page_slot_index,
    memory_state,
    retention,
    momentum,
    memory_step_scale,
    halving_updates,
):
    shard_tokens = tokens.shape[1]
    width = tokens.shape[2]
    cols = projection_weight.shape[2]
    devices = cache_page_slots.shape[1]
    span = cache_page_slots.shape[2]
    lanes = span // PAGE
    max_pages = page_keeper.shape[1]
    planes = devices // GROUP
    n_head = lax.axis_size("head")
    here = lax.axis_index("req")
    plane, place = here // GROUP, here % GROUP
    side = lax.axis_index("head")

    def swap(value, step):
        return lax.ppermute(value, "req", [(i, i ^ step) for i in range(devices)])

    def turn(value, step):
        return lax.ppermute(
            value, "head", [(i, (i - step) % n_head) for i in range(n_head)]
        )

    def projection(rows, weight):
        return dot(weight, rows, ((0,), (1,)))

    def norm(rows):
        x = rows.astype(f32)
        return (
            x * lax.rsqrt(jnp.mean(x * x, axis=-1, keepdims=True) + norm_eps) * gain.astype(f32)
        ).astype(bf16)

    def ordered(value, *earlier):
        return lax.optimization_barrier((value,) + earlier)[0]

    others = [turn(tokens[0], step) for step in range(1, n_head)]

    page_ids = jnp.arange(max_pages, dtype=jnp.int32)
    filled = jnp.clip(cached_length[0] - page_ids * PAGE, 0, PAGE)
    slot_of = page_keeper[0] * lanes + page_slot_index[0]
    keeper = (plane ^ jnp.arange(planes, dtype=jnp.int32))[:, None] * GROUP + (
        place ^ jnp.arange(GROUP, dtype=jnp.int32)
    )
    slot_ids = keeper[:, :, None] * lanes + jnp.arange(lanes, dtype=jnp.int32)
    slot_fill = jnp.sum(
        jnp.where(slot_of == slot_ids[..., None], filled, 0), axis=-1
    )

    offsets = list(range(2, planes)) + [1, 0]
    core = place % 2
    cache = cache_page_slots[0]
    heads = cols // HD
    cache = cache.reshape(devices, span, 2, heads, HD).transpose(0, 1, 3, 2, 4)
    cache = cache.reshape(devices, span * heads * 2, HD)

    hands = []
    for d in offsets:
        start = (plane ^ d) * GROUP + ((place // 2) ^ 1) * 2
        hands.append([start, start + 1])
    for k in (1, 0):
        hands.append([z * GROUP + (place ^ k) for z in range(planes)])
    pieces = dict(zip(offsets, deal(cache, hands[:1], gain, 56 * 2**20)))

    def with_fill(value, d):
        rows = jnp.concatenate([slot_fill[d], slot_fill[d ^ 1]], axis=0)
        tail = TAIL if d == 1 else 2 * TAIL
        rows = jnp.pad(rows, ((0, tail - 2 * GROUP), (0, value.shape[1] - lanes)))
        return jnp.concatenate([value, rows.astype(bf16)], axis=0)

    across, sibling, far_here, far_rest = {}, {}, {}, {}

    def pass_on(d, *earlier):
        piece = ordered(across[d], *earlier)
        if d:
            (piece,) = deal(piece, [[1 - core]], gain, 2 * 2**20)
        else:
            piece = lax.dynamic_index_in_dim(piece, 1 - core, 0)
        sibling[d] = swap(piece, 1)

    first, second = offsets[:2]
    across[first] = swap(pieces[first], 2)
    flat = ordered(projection_weight, pieces[first]).reshape(width, 4 * cols)
    normed_here = norm(tokens[0])
    query_here = projection(normed_here, flat[:, :cols]).astype(bf16)
    far_here[first] = swap(with_fill(query_here, first), first * GROUP)
    far_here[1] = swap(with_fill(query_here, 1), GROUP)
    normed_rest = norm(ordered(jnp.concatenate(others, axis=0), query_here))
    query_rest = projection(normed_rest, flat[:, :cols]).astype(bf16)
    far_rest[first] = swap(query_rest, first * GROUP)
    *rest, column, own = deal(cache, hands[1:], query_rest, 56 * 2**20)
    pieces |= zip(offsets[1:], rest)
    across[second] = swap(pieces[second], 2)
    beside = swap(column, 1)
    projected = projection(
        jnp.concatenate([normed_here, normed_rest], axis=0), ordered(flat, query_rest)[:, cols:]
    )
    queries = jnp.concatenate([query_here, query_rest], axis=1)
    own_keys = projected[:cols].astype(bf16)
    own_values = projected[cols : 2 * cols].astype(bf16)
    far_rest[1] = swap(ordered(query_rest, far_here[1], own_values), GROUP)

    att, lse = own_attention(side, shard_tokens, queries, own_keys, own_values, persist)
    near, far = [(att, lse)], []
    fill_here = jnp.pad(slot_fill[0], ((0, TAIL - GROUP), (0, HD - lanes))).astype(bf16)
    pass_on(first, lse)

    def whole_of(d):
        rest_rows = ((0, far_here[d].shape[0] - cols), (0, 0))
        rest_rows = jnp.pad(far_rest[d], rest_rows)
        return jnp.concatenate([far_here[d], rest_rows], axis=1)

    asked = {}
    done = fence(lse)
    for i, d in enumerate(offsets):
        if i and d:
            pass_on(d, done)
        if d == 1:
            asked[1] = whole_of(1)
        if d and d % 2 == 0:
            if d not in far_here:
                far_here[d] = swap(with_fill(ordered(query_here, done), d), d * GROUP)
                far_rest[d] = swap(ordered(query_rest, done), d * GROUP)
            asked[d] = whole_of(d)
            asked[d ^ 1] = swap(asked[d], GROUP)
        if i + 2 < len(offsets):
            earlier = [across[d], far_here[d], far_rest[d]] if i == 0 else [done, far_rest[1]]
            across[offsets[i + 2]] = swap(ordered(pieces[offsets[i + 2]], *earlier), 2)
        kvs = [own, beside, across[d], sibling.get(d)]
        at = [plane ^ d, plane ^ d, core, jnp.zeros_like(core)]
        if d:
            if d != first:
                done = fence(done)
            row = GROUP * (d % 2 if d > 1 else 0)
            (done,) = cache_attention(
                asked[d], cols, asked[d], row, kvs, at, True, done
            )
            far.append(swap(done, d * GROUP))
            if i == len(offsets) - 3:
                weights = [output_weight] + [
                    turn(ordered(output_weight, done), step) for step in range(1, n_head)
                ]
        else:
            pair = cache_attention(
                queries, cols, fill_here, 0, kvs[:2], at[:2], False, done
            )
            near.append(pair)
            done = fence(pair[1], far[0])
            pass_on(d, done)
            kvs[3] = sibling[d]
            for part in (slice(2, 3), slice(3, 4)):
                pair = cache_attention(
                    queries, cols, fill_here, part.start, kvs[part], at[part], False, done
                )
                near.append(pair)
                done = pair[1]
        if i == 0:
            memory_read, new_state = memory_pass(
                side, shard_tokens, retention, momentum, memory_step_scale, halving_updates,
                done, queries, own_keys, own_values, memory_state[:, 0],
            )
            done = memory_read
    head_out = merge(near, far, projected, memory_read)

    layer = jnp.zeros((shard_tokens, width), f32)
    for step in range(n_head):
        away = (n_head - step) % n_head
        part = head_out[:, away * shard_tokens : (away + 1) * shard_tokens]
        if step:
            part = turn(part, step)
        layer = layer + dot(part, weights[step], ((0,), (0,))).astype(bf16).astype(f32)
    return (layer.astype(bf16)[None], new_state[:, None])


def solution(mesh):
    in_specs = (
        P("req", "head", None),
        P(),
        P(None, None, "head"),
        P("head", None),
        P(None, None, "head"),
        P("req", None, None, None, "head"),
        P("req"),
        P("req", None),
        P("req", None),
        P(None, "req", "head", None, None),
        P("req", "head"),
        P("req", "head"),
        P("req", "head"),
        P("req", None),
    )
    out_specs = (P("req", "head", None), P(None, "req", "head", None, None))
    return jax.shard_map(shards, mesh=mesh, in_specs=in_specs, out_specs=out_specs, check_vma=False)
```

```python
import functools
import math

import jax
import jax.numpy as jnp
from jax import lax
from jax.experimental import pallas as pl
from jax.experimental.pallas import tpu as pltpu
from jax.sharding import PartitionSpec as P

HD = 128
BLK = 64
PAGE = 32
GROUP = 4


norm_eps = 1e-05
unit_eps = 1e-06
LOG2E = math.log2(math.e)
MASKED = -1e30
LAST = pl.CostEstimate(flops=6 * 10**9, bytes_accessed=1, transcendentals=0)
VMEM_LIMIT = 16 * 2**20
TAIL = 16
f32 = jnp.float32
bf16 = jnp.bfloat16
COST = pl.CostEstimate(flops=1, bytes_accessed=1, transcendentals=0)


def dot(left, right, contract=((1,), (0,)), precision=None):
    return lax.dot_general(
        left, right, (contract, ((), ())), precision=precision, preferred_element_type=f32
    )


def fence_kernel(*refs):
    refs[-1][...] = jnp.zeros_like(refs[-1])


def fence(*earlier):
    return pl.pallas_call(
        fence_kernel,
        out_shape=jax.ShapeDtypeStruct((8, HD), f32),
        in_specs=[pl.BlockSpec(memory_space=pl.ANY)] * len(earlier),
        compiler_params=pltpu.CompilerParams(vmem_limit_bytes=2**20),
        cost_estimate=LAST,
    )(*earlier)


def deal_kernel(choose, from_ref, after_ref, *refs):
    del after_ref
    hands = choose(lax.axis_index("req"))
    outs, (held, into, out_of) = refs[: len(hands)], refs[len(hands) :]
    places = [(out, i, row) for hand, out in zip(hands, outs) for i, row in enumerate(hand)]
    reads, writes = [], []
    for at, (out, i, row) in enumerate(places):
        reads.append(pltpu.make_async_copy(from_ref.at[row], held.at[at], into.at[at]))
        writes.append(pltpu.make_async_copy(held.at[at], out.at[i], out_of.at[at]))
    for copy in reads:
        copy.start()
    for read, write in zip(reads, writes):
        read.wait()
        write.start()
    for copy in writes:
        copy.wait()


def deal(source, choose, after, vmem_limit):
    counts = [len(hand) for hand in choose(0)]
    total = sum(counts)
    anywhere = pl.BlockSpec(memory_space=pl.ANY)
    return pl.pallas_call(
        functools.partial(deal_kernel, choose),
        out_shape=[
            jax.ShapeDtypeStruct((count,) + source.shape[1:], source.dtype) for count in counts
        ],
        in_specs=[anywhere] * 2,
        out_specs=[anywhere] * len(counts),
        scratch_shapes=[
            pltpu.VMEM((total,) + source.shape[1:], source.dtype),
            pltpu.SemaphoreType.DMA((total,)),
            pltpu.SemaphoreType.DMA((total,)),
        ],
        compiler_params=pltpu.CompilerParams(vmem_limit_bytes=vmem_limit),
        cost_estimate=COST,
    )(source, after)


def cache_kernel(shape, sent, at_ref, after_ref, q_ref, fill_ref, *refs):
    del after_ref
    span, heads, count, fill_row = shape
    kv_refs = refs[:count]
    outs = refs[count:-6]
    kept_ref, wide_ref, bias_ref, score_ref, tail_ref, sems = refs[-6:]
    scale = LOG2E / math.sqrt(HD)
    head = pl.program_id(0)

    @pl.when(head == 0)
    def _():
        copies = [
            pltpu.make_async_copy(kv_refs[g].at[at_ref[g]], kept_ref.at[g], sems.at[g])
            for g in range(count)
        ]
        for copy in copies:
            copy.start()
        row = lax.broadcasted_iota(jnp.int32, (span, HD), 0)
        lane = lax.broadcasted_iota(jnp.int32, (span, HD), 1)
        slot = jnp.where(row // PAGE == lane, 1.0, 0.0).astype(bf16)
        filled = dot(slot, fill_ref[...], ((1,), (1,)))
        row_f = (row % PAGE).astype(f32)
        tail_ref[...] = jnp.zeros_like(tail_ref)
        for g in range(count):
            column = filled[:, fill_row + g : fill_row + g + 1]
            bias_ref[pl.ds(g * span, span), :] = jnp.where(row_f < column, 0.0, MASKED)
            copies[g].wait()
            wide_ref[g, pl.ds(0, 2 * heads * span), :] = kept_ref[g].astype(f32)

    def part_of(g, which):
        rows = pl.ds(2 * head + which, span, stride=2 * heads)
        return wide_ref[g, rows, :].astype(bf16)

    q = q_ref[...]
    tokens = q.shape[1]
    top = jnp.full((1, tokens), MASKED, f32)
    for g in range(count):
        rows = pl.ds(g * span, span)
        score = dot(part_of(g, 0), q) * scale + jnp.tile(bias_ref[rows, :], (1, tokens // HD))
        score_ref[rows, :] = score
        top = jnp.maximum(top, jnp.max(score, axis=0, keepdims=True))
    total = jnp.zeros((1, tokens), f32)
    mixed = jnp.zeros((HD, tokens), f32)
    for g in range(count):
        rows = pl.ds(g * span, span)
        weight = jnp.exp2(score_ref[rows, :] - top)
        total = total + jnp.sum(weight, axis=0, keepdims=True)
        mixed = mixed + dot(part_of(g, 1), weight.astype(bf16), ((0,), (0,)))
    attended = mixed / total
    lse = top + jnp.log2(total)
    if sent:
        (out,) = outs
        rows = pl.ds(pl.multiple_of(head * HD, HD), HD)
        out[rows, :] = attended.astype(bf16)
        high = lse.astype(bf16).astype(f32)
        middle = (lse - high).astype(bf16).astype(f32)
        for i, term in enumerate((high, middle, lse - high - middle)):
            tail_ref[pl.ds(i * heads + head, 1), :] = term

        @pl.when(head == heads - 1)
        def _():
            out[pl.ds(heads * HD, TAIL), :] = tail_ref[...].astype(bf16)
    else:
        outs[0][0] = attended
        outs[1][0] = lse


def cache_attention(queries, cols, fill, fill_row, kvs, at, sent, after):
    count = len(kvs)
    heads = cols // HD
    span = kvs[0].shape[1] // (2 * heads)
    tokens = queries.shape[1]
    fill_at = cols // TAIL if fill.shape[0] > TAIL else 0

    def head_spec(*block):
        return pl.BlockSpec((1,) + block, lambda h, at: (h, 0, 0))

    if sent:
        out_shape = (jax.ShapeDtypeStruct((cols + TAIL, tokens), bf16),)
        out_specs = (pl.BlockSpec((cols + TAIL, tokens), lambda h, at: (0, 0)),)
    else:
        out_shape = (
            jax.ShapeDtypeStruct((heads, HD, tokens), f32),
            jax.ShapeDtypeStruct((heads, 1, tokens), f32),
        )
        out_specs = (head_spec(HD, tokens), head_spec(1, tokens))
    return pl.pallas_call(
        functools.partial(cache_kernel, (span, heads, count, fill_row), sent),
        out_shape=out_shape,
        grid_spec=pltpu.PrefetchScalarGridSpec(
            num_scalar_prefetch=1,
            grid=(heads,),
            in_specs=[
                pl.BlockSpec(memory_space=pl.ANY),
                pl.BlockSpec((HD, tokens), lambda h, at: (h, 0)),
                pl.BlockSpec((TAIL, HD), lambda h, at: (fill_at, 0)),
            ]
            + [pl.BlockSpec(memory_space=pl.ANY)] * count,
            out_specs=out_specs,
            scratch_shapes=[
                pltpu.VMEM((count,) + kvs[0].shape[1:], bf16),
                pltpu.VMEM((count, 2 * heads * (span + 1), HD), f32),
                pltpu.VMEM((count * span, HD), f32),
                pltpu.VMEM((count * span, tokens), f32),
                pltpu.VMEM((TAIL, tokens), f32),
                pltpu.SemaphoreType.DMA((count,)),
            ],
        ),
        compiler_params=pltpu.CompilerParams(vmem_limit_bytes=VMEM_LIMIT),
        cost_estimate=COST,
    )(jnp.stack(at), after, queries, fill, *kvs)


def own_kernel(shard, shards_in_all, side_ref, q_ref, k_ref, v_ref, persist_ref, att_ref, lse_ref):
    def place(axis):
        at = lax.broadcasted_iota(jnp.int32, (tokens, tokens), axis)
        return lax.rem(side_ref[0] + at // shard, shards_in_all) * shard + lax.rem(at, shard)

    scale = LOG2E / math.sqrt(HD)
    q = q_ref[...]
    tokens = q.shape[1]
    score_p = dot(persist_ref[0], q) * scale
    score_t = dot(k_ref[...].T, q) * scale
    score_t = jnp.where(place(0) <= place(1), score_t, MASKED)
    top = jnp.maximum(
        jnp.max(score_p, axis=0, keepdims=True), jnp.max(score_t, axis=0, keepdims=True)
    )
    weight_p = jnp.exp2(score_p - top)
    weight_t = jnp.exp2(score_t - top)
    total = jnp.sum(weight_p, axis=0, keepdims=True) + jnp.sum(weight_t, axis=0, keepdims=True)
    mixed = dot(v_ref[...], weight_t.astype(bf16)) + dot(
        persist_ref[1], weight_p.astype(bf16), ((0,), (0,))
    )
    att_ref[0] = mixed / total
    lse_ref[0] = top + jnp.log2(total)


def own_attention(side, shard, q, k, v, persist):
    cols, tokens = q.shape
    heads = cols // HD
    head_spec = pl.BlockSpec((HD, tokens), lambda h: (h, 0))
    return pl.pallas_call(
        functools.partial(own_kernel, shard, tokens // shard),
        out_shape=(
            jax.ShapeDtypeStruct((heads, HD, tokens), f32),
            jax.ShapeDtypeStruct((heads, 1, tokens), f32),
        ),
        grid=(heads,),
        in_specs=[pl.BlockSpec(memory_space=pltpu.SMEM)]
        + [head_spec] * 3
        + [pl.BlockSpec((2, persist.shape[1], HD), lambda h: (0, 0, h))],
        out_specs=(
            pl.BlockSpec((1, HD, tokens), lambda h: (h, 0, 0)),
            pl.BlockSpec((1, 1, tokens), lambda h: (h, 0, 0)),
        ),
        compiler_params=pltpu.CompilerParams(vmem_limit_bytes=VMEM_LIMIT),
        cost_estimate=COST,
    )(side[None], q, k, v, persist)


def memory_kernel(
    shards_in_all, side_ref, retention_ref, momentum_ref, step_ref, halving_ref, after_ref,
    q_ref, k_ref, v_ref, state_ref, read_ref, new_ref, kn_ref,
):
    del after_ref
    heads = state_ref.shape[1]
    tokens = q_ref.shape[1]
    shard = tokens // shards_in_all
    exact = lax.Precision.HIGHEST
    ms = [state_ref[0, h] for h in range(heads)]
    ss = [state_ref[1, h] for h in range(heads)]
    for a in range(shards_in_all):
        start = lax.rem(a + shards_in_all - side_ref[0], shards_in_all) * shard
        lanes = slice(None) if shards_in_all == 1 else pl.ds(pl.multiple_of(start, HD), shard)
        units = []
        for h in range(heads):
            rows = pl.ds(h * HD, HD)
            q = q_ref[rows, lanes].astype(f32)
            k = k_ref[rows, lanes].astype(f32)
            qn = q * lax.rsqrt(jnp.sum(q * q, axis=0, keepdims=True) + unit_eps)
            kn = k * lax.rsqrt(jnp.sum(k * k, axis=0, keepdims=True) + unit_eps)
            kn_ref[h] = kn.T
            units.append((qn, kn, v_ref[rows, lanes].astype(f32), []))
        for b in range(shard // BLK):
            lower, upper = b * BLK, (b + 1) * BLK
            for h in range(heads):
                qn, kn, values, reads = units[h]
                both = jnp.concatenate([kn[:, lower:upper], qn[:, lower:upper]], axis=1)
                product = dot(ms[h], both, precision=exact)
                error = product[:, :BLK] - values[:, lower:upper]
                reads.append(product[:, BLK:])
                grad = dot(error, kn_ref[h, lower:upper, :], precision=exact)
                ss[h] = momentum_ref[0, h] * ss[h] - step_ref[0, h] * grad
                halving = halving_ref[0, a * (shard // BLK) + b]
                keep = retention_ref[0, h] * jnp.where(halving == 1, 0.5, 1.0)
                ms[h] = keep * ms[h] + ss[h]
        for h in range(heads):
            read_ref[pl.ds(h * HD, HD), lanes] = jnp.concatenate(units[h][3], axis=1)
    for h in range(heads):
        new_ref[0, h] = ms[h]
        new_ref[1, h] = ss[h]


def memory_pass(side, shard, retention, momentum, step, halving, after, q, k, v, state):
    cols, tokens = q.shape
    heads = cols // HD
    count = tokens // shard if shard % HD == 0 else 1

    def rolled(value, shift):
        twice = jnp.concatenate([value, value], axis=1)
        return lax.dynamic_slice_in_dim(twice, shift * shard, tokens, 1)

    if count == 1:
        back = (tokens // shard - side) % (tokens // shard)
        q, k, v = rolled(q, back), rolled(k, back), rolled(v, back)
    smem = pl.BlockSpec(memory_space=pltpu.SMEM)
    vmem = pl.BlockSpec(memory_space=pltpu.VMEM)
    read, new = pl.pallas_call(
        functools.partial(memory_kernel, count),
        out_shape=(
            jax.ShapeDtypeStruct((cols, tokens), f32),
            jax.ShapeDtypeStruct(state.shape, f32),
        ),
        in_specs=[smem] * 5 + [pl.BlockSpec(memory_space=pl.ANY)] + [vmem] * 4,
        out_specs=(vmem, vmem),
        scratch_shapes=[pltpu.VMEM((heads, tokens // count, HD), f32)],
        compiler_params=pltpu.CompilerParams(vmem_limit_bytes=VMEM_LIMIT),
        cost_estimate=COST,
    )(side[None], retention, momentum, step, halving, after, q, k, v, state)
    return (read if count > 1 else rolled(read, side)), new


def merge_kernel(near, heads, *refs):
    pairs = [(refs[2 * i][0], refs[2 * i + 1][0]) for i in range(near)]
    for att, tail in zip(refs[2 * near : -3 : 2], refs[2 * near + 1 : -3 : 2]):
        row = lax.broadcasted_iota(jnp.int32, tail.shape, 0)
        mine = (lax.rem(row, heads) == pl.program_id(0)) & (row < 3 * heads)
        lse = jnp.sum(jnp.where(mine, tail[...].astype(f32), 0.0), axis=0, keepdims=True)
        pairs.append((att[...].astype(f32), lse))
    gate_ref, read_ref, out_ref = refs[-3:]
    top = functools.reduce(jnp.maximum, [lse for _, lse in pairs])
    total = jnp.zeros_like(top)
    mixed = jnp.zeros(out_ref.shape, f32)
    for att, lse in pairs:
        share = jnp.exp2(lse - top)
        total = total + share
        mixed = mixed + att * share
    attended = mixed / total
    unit = attended * lax.rsqrt(jnp.mean(attended * attended, axis=0, keepdims=True) + unit_eps)
    gate = 1.0 / (1.0 + jnp.exp(-gate_ref[...]))
    out_ref[...] = (unit + gate * read_ref[...]).astype(bf16)


def merge(near, far, projected, read):
    cols, tokens = read.shape
    heads = cols // HD
    gates = projected.shape[0] // HD - heads
    flat_spec = pl.BlockSpec((HD, tokens), lambda h: (h, 0))

    def head_spec(*block):
        return pl.BlockSpec((1,) + block, lambda h: (h, 0, 0))

    return pl.pallas_call(
        functools.partial(merge_kernel, len(near), heads),
        out_shape=jax.ShapeDtypeStruct((cols, tokens), bf16),
        grid=(heads,),
        in_specs=[head_spec(HD, tokens), head_spec(1, tokens)] * len(near)
        + [flat_spec, pl.BlockSpec((TAIL, tokens), lambda h: (cols // TAIL, 0))] * len(far)
        + [pl.BlockSpec((HD, tokens), lambda h: (gates + h, 0)), flat_spec],
        out_specs=flat_spec,
        compiler_params=pltpu.CompilerParams(vmem_limit_bytes=VMEM_LIMIT),
        cost_estimate=pl.CostEstimate(
            flops=10 * (len(near) + len(far)) * cols * tokens,
            bytes_accessed=(4 * len(near) + 2 * len(far) + 10) * cols * tokens,
            transcendentals=cols * tokens,
        ),
    )(*(value for pair in near for value in pair), *(f for f in far for _ in (0, 1)), projected, read)


def shards(
    tokens,
    gain,
    projection_weight,
    output_weight,
    persist,
    cache_page_slots,
    cached_length,
    page_keeper,
    page_slot_index,
    memory_state,
    retention,
    momentum,
    memory_step_scale,
    halving_updates,
):
    shard_tokens = tokens.shape[1]
    width = tokens.shape[2]
    cols = projection_weight.shape[2]
    devices = cache_page_slots.shape[1]
    span = cache_page_slots.shape[2]
    lanes = span // PAGE
    max_pages = page_keeper.shape[1]
    planes = devices // GROUP
    n_head = lax.axis_size("head")
    here = lax.axis_index("req")
    plane, place = here // GROUP, here % GROUP
    side = lax.axis_index("head")

    def swap(value, step):
        return lax.ppermute(value, "req", [(i, i ^ step) for i in range(devices)])

    def turn(value, step):
        return lax.ppermute(
            value, "head", [(i, (i - step) % n_head) for i in range(n_head)]
        )

    def projection(rows, weight):
        return dot(weight, rows, ((0,), (1,)))

    def norm(rows):
        x = rows.astype(f32)
        return (
            x * lax.rsqrt(jnp.mean(x * x, axis=-1, keepdims=True) + norm_eps) * gain.astype(f32)
        ).astype(bf16)

    def ordered(value, *earlier):
        return lax.optimization_barrier((value,) + earlier)[0]

    others = [turn(tokens[0], step) for step in range(1, n_head)]

    page_ids = jnp.arange(max_pages, dtype=jnp.int32)
    filled = jnp.clip(cached_length[0] - page_ids * PAGE, 0, PAGE)
    slot_of = page_keeper[0] * lanes + page_slot_index[0]
    keeper = (plane ^ jnp.arange(planes, dtype=jnp.int32))[:, None] * GROUP + (
        place ^ jnp.arange(GROUP, dtype=jnp.int32)
    )
    slot_ids = keeper[:, :, None] * lanes + jnp.arange(lanes, dtype=jnp.int32)
    slot_fill = jnp.sum(
        jnp.where(slot_of == slot_ids[..., None], filled, 0), axis=-1
    )

    offsets = list(range(2, planes)) + [1, 0]
    core = place % 2
    cache = cache_page_slots[0]
    heads = cols // HD
    cache = cache.reshape(devices, span, 2, heads, HD).transpose(0, 1, 3, 2, 4)
    cache = cache.reshape(devices, span * heads * 2, HD)

    def hands(here):
        plane, place = here // GROUP, here % GROUP
        rows = []
        for d in offsets:
            start = (plane ^ d) * GROUP + ((place // 2) ^ 1) * 2
            rows.append([start, start + 1])
        for k in (1, 0):
            rows.append([z * GROUP + (place ^ k) for z in range(planes)])
        return rows

    pieces = dict(zip(offsets, deal(cache, lambda here: hands(here)[:1], gain, 56 * 2**20)))

    def with_fill(value, d):
        rows = jnp.concatenate([slot_fill[d], slot_fill[d ^ 1]], axis=0)
        tail = TAIL if d == 1 else 2 * TAIL
        rows = jnp.pad(rows, ((0, tail - 2 * GROUP), (0, value.shape[1] - lanes)))
        return jnp.concatenate([value, rows.astype(bf16)], axis=0)

    across, sibling, far_here, far_rest = {}, {}, {}, {}

    def pass_on(d, *earlier):
        piece = ordered(across[d], *earlier)
        if d:
            (piece,) = deal(piece, lambda here: [[1 - here % 2]], gain, 2 * 2**20)
        else:
            piece = lax.dynamic_index_in_dim(piece, 1 - core, 0)
        sibling[d] = swap(piece, 1)

    first, second = offsets[:2]
    across[first] = swap(pieces[first], 2)
    flat = ordered(projection_weight, pieces[first]).reshape(width, 4 * cols)
    normed_here = norm(tokens[0])
    query_here = projection(normed_here, flat[:, :cols]).astype(bf16)
    far_here[first] = swap(with_fill(query_here, first), first * GROUP)
    far_here[1] = swap(with_fill(query_here, 1), GROUP)
    normed_rest = norm(ordered(jnp.concatenate(others, axis=0), query_here))
    query_rest = projection(normed_rest, flat[:, :cols]).astype(bf16)
    far_rest[first] = swap(query_rest, first * GROUP)
    *rest, column, own = deal(cache, lambda here: hands(here)[1:], query_rest, 56 * 2**20)
    pieces |= zip(offsets[1:], rest)
    across[second] = swap(pieces[second], 2)
    beside = swap(column, 1)
    projected = projection(
        jnp.concatenate([normed_here, normed_rest], axis=0), ordered(flat, query_rest)[:, cols:]
    )
    queries = jnp.concatenate([query_here, query_rest], axis=1)
    own_keys = projected[:cols].astype(bf16)
    own_values = projected[cols : 2 * cols].astype(bf16)
    far_rest[1] = swap(ordered(query_rest, far_here[1], own_values), GROUP)

    att, lse = own_attention(side, shard_tokens, queries, own_keys, own_values, persist)
    near, far = [(att, lse)], []
    fill_here = jnp.pad(slot_fill[0], ((0, TAIL - GROUP), (0, HD - lanes))).astype(bf16)
    pass_on(first, lse)

    def whole_of(d):
        rest_rows = ((0, far_here[d].shape[0] - cols), (0, 0))
        rest_rows = jnp.pad(far_rest[d], rest_rows)
        return jnp.concatenate([far_here[d], rest_rows], axis=1)

    asked = {}
    done = fence(lse)
    for i, d in enumerate(offsets):
        if i and d:
            pass_on(d, done)
        if d == 1:
            asked[1] = whole_of(1)
        if d and d % 2 == 0:
            if d not in far_here:
                far_here[d] = swap(with_fill(ordered(query_here, done), d), d * GROUP)
                far_rest[d] = swap(ordered(query_rest, done), d * GROUP)
            asked[d] = whole_of(d)
            asked[d ^ 1] = swap(asked[d], GROUP)
        if i + 2 < len(offsets):
            earlier = [across[d], far_here[d], far_rest[d]] if i == 0 else [done, far_rest[1]]
            across[offsets[i + 2]] = swap(ordered(pieces[offsets[i + 2]], *earlier), 2)
        kvs = [own, beside, across[d], sibling.get(d)]
        at = [plane ^ d, plane ^ d, core, jnp.zeros_like(core)]
        if d:
            if d != first:
                done = fence(done)
            row = GROUP * (d % 2 if d > 1 else 0)
            (done,) = cache_attention(
                asked[d], cols, asked[d], row, kvs, at, True, done
            )
            far.append(swap(done, d * GROUP))
            if i == len(offsets) - 3:
                weights = [output_weight] + [
                    turn(ordered(output_weight, done), step) for step in range(1, n_head)
                ]
        else:
            pair = cache_attention(
                queries, cols, fill_here, 0, kvs[:2], at[:2], False, done
            )
            near.append(pair)
            done = fence(pair[1], far[0])
            pass_on(d, done)
            kvs[3] = sibling[d]
            for part in (slice(2, 3), slice(3, 4)):
                pair = cache_attention(
                    queries, cols, fill_here, part.start, kvs[part], at[part], False, done
                )
                near.append(pair)
                done = pair[1]
        if i == 0:
            memory_read, new_state = memory_pass(
                side, shard_tokens, retention, momentum, memory_step_scale, halving_updates,
                done, queries, own_keys, own_values, memory_state[:, 0],
            )
            done = memory_read
    head_out = merge(near, far, projected, memory_read)

    layer = jnp.zeros((shard_tokens, width), f32)
    for step in range(n_head):
        away = (n_head - step) % n_head
        part = head_out[:, away * shard_tokens : (away + 1) * shard_tokens]
        if step:
            part = turn(part, step)
        layer = layer + dot(part, weights[step], ((0,), (0,))).astype(bf16).astype(f32)
    return (layer.astype(bf16)[None], new_state[:, None])


def solution(mesh):
    in_specs = (
        P("req", "head", None),
        P(),
        P(None, None, "head"),
        P("head", None),
        P(None, None, "head"),
        P("req", None, None, None, "head"),
        P("req"),
        P("req", None),
        P("req", None),
        P(None, "req", "head", None, None),
        P("req", "head"),
        P("req", "head"),
        P("req", "head"),
        P("req", None),
    )
    out_specs = (P("req", "head", None), P(None, "req", "head", None, None))
    return jax.shard_map(shards, mesh=mesh, in_specs=in_specs, out_specs=out_specs, check_vma=False)
```
